256 devices in a mesh: sec: 4 (over y), dom: 64 (over x, z, core).
Axes of the slice: x: 4, y: 4, z: 8, core: 2. Of those that a mesh axis runs over, the one named last changes fastest.
Arguments:
- defect: float32 [5, 64, 16, 8192], P(None, None, 'sec', 'dom'), may hold values from -6 to 6
- point_inverse: float32 [5, 5, 64, 16, 8192], P(None, None, None, 'sec', 'dom'), may hold values from -0.04 to 0.25
- flux_jacobian: float32 [3, 5, 5, 16, 8192], P(None, None, None, 'sec', 'dom'), may hold values from -1 to 1
- time_term: float32 [16, 8192], P('sec', 'dom'), may hold values from 2 to 4
- penalty: float32 [3, 16, 8192], P(None, 'sec', 'dom'), may hold values from 0.5 to 2
- element_inverse: float32 [5, 5, 16, 8192], P(None, None, 'sec', 'dom'), may hold values from -0.04 to 0.25
Outputs:
- correction: float32 [5, 64, 16, 8192], P(None, None, 'sec', 'dom')
The draws below stay inside these ranges and needn't reach their ends.
All inputs are finite; a program needn't handle non-finite values.
Results may differ from the reference program's by a relative error of at most 0.0001.
Values sent between devices are 32-bit elements; how exact they have to be, the bound alone decides.
A program may use at most 64 MiB of HBM per device.

```python
import math
import jax
import jax.numpy as jnp
import numpy as np
from jax import lax

VARS = 5
NODES = 64
EZ = 32
NX = 256
NY = 16


def identity_mask(shape):
    return (lax.broadcasted_iota(jnp.int32, shape, 0) == lax.broadcasted_iota(jnp.int32, shape, 1)).astype(jnp.float32)


def draw_point_inverse(key, part):
    key = jax.random.fold_in(key, 11)
    shape = (5, 5, NODES, NY, NX * EZ)
    first_key, second_key = jax.random.split(key)
    identity = identity_mask(shape)
    diagonal = jnp.exp(jax.random.uniform(first_key, shape, jnp.float32, math.log(0.12), math.log(0.25)))
    off_diagonal = jax.random.uniform(second_key, shape, jnp.float32, -0.04, 0.04)
    return identity * diagonal + (1.0 - identity) * off_diagonal


def draw_element_inverse(key, part):
    key = jax.random.fold_in(key, 23)
    shape = (5, 5, NY, NX * EZ)
    first_key, second_key = jax.random.split(key)
    identity = identity_mask(shape)
    diagonal = jnp.exp(jax.random.uniform(first_key, shape, jnp.float32, math.log(0.12), math.log(0.25)))
    off_diagonal = jax.random.uniform(second_key, shape, jnp.float32, -0.04, 0.04)
    return identity * diagonal + (1.0 - identity) * off_diagonal


def block_scale(own_key, extent, pieces, smallest, top_value):
    def one(dim, shards_of):
        steps = jax.random.uniform(jax.random.fold_in(jax.random.fold_in(own_key, 6), dim), (shards_of,), jnp.float32, smallest / len(pieces), top_value / len(pieces))
        return jnp.repeat(jnp.exp(steps), extent[dim] // shards_of).reshape((-1,) + (1,) * (len(extent) - dim - 1))

    factor_of = one(*pieces[0])
    for cut in pieces[1:]:
        factor_of = factor_of * one(*cut)
    return factor_of


def scatter_about(own_key, shape, spread, most, cuts=(), dtype=jnp.bfloat16):
    values = spread * jax.random.normal(own_key, shape, jnp.float32)
    if cuts:
        values = values * block_scale(own_key, shape, cuts, -0.22, 0.18)
    return jnp.clip(values, -most, most).astype(dtype)


def setup_inputs(seed: int = 0) -> dict:
    keys = jax.random.split(jax.random.key(seed), 7)
    defect = scatter_about(keys[0], (VARS, NODES, NY, NX * EZ), 1.0, 6.0, ((2, 4), (3, 64)), jnp.float32)
    point_inverse = draw_point_inverse(jax.random.fold_in(keys[6], 71), 0)
    flux_jacobian = scatter_about(keys[2], (3, VARS, VARS, NY, NX * EZ), 0.2, 1.0, ((3, 4), (4, 64)), jnp.float32)
    time_term = jnp.clip(2.0 + 2.0 * jax.random.uniform(keys[3], (NY, NX * EZ), jnp.float32) ** block_scale(keys[3], (NY, NX * EZ), ((0, 4), (1, 64)), -0.2, 0.2), 2.0, 4.0)
    penalty = jnp.clip(jnp.exp(math.log(2.0) - 1.3862944 * jax.random.uniform(keys[4], (3, NY, NX * EZ), jnp.float32) ** block_scale(keys[4], (3, NY, NX * EZ), ((1, 4), (2, 64)), -0.2, 0.2)), 0.5, 2.0)
    element_inverse = draw_element_inverse(jax.random.fold_in(keys[6], 71), 0)
    return {"defect": defect, "point_inverse": point_inverse, "flux_jacobian": flux_jacobian, "time_term": time_term, "penalty": penalty, "element_inverse": element_inverse}


DAMPING = 0.7

def node_tables():
    points = np.array([-1.0, -1.0 / np.sqrt(5.0), 1.0 / np.sqrt(5.0), 1.0])
    barycentric = np.array([1.0 / np.prod([points[j] - points[k] for k in range(4) if k != j]) for j in range(4)])
    derivative = np.zeros((4, 4))
    for i in range(4):
        for j in range(4):
            if i != j:
                derivative[i, j] = barycentric[j] / barycentric[i] / (points[i] - points[j])
        derivative[i, i] = -np.sum(derivative[i])
    coarse_derivative = np.array([[-0.5, 0.5], [-0.5, 0.5]])
    interpolate = np.stack([(1.0 - points) / 2.0, (1.0 + points) / 2.0], axis=1)
    return (derivative, coarse_derivative, interpolate)

def along_axis(matrix, values, axis):
    patterns = {1: 'pq,aqjkyl->apjkyl', 2: 'pq,aiqkyl->aipkyl', 3: 'pq,aijqyl->aijpyl'}
    return jnp.einsum(patterns[axis], jnp.asarray(matrix, jnp.float32), values, precision=lax.Precision.HIGHEST)

def three_axes(matrix, values):
    for axis in (1, 2, 3):
        values = along_axis(matrix, values, axis)
    return values

def block_product(blocks, vector):
    total = blocks[:, 0] * vector[0][None]
    for column in range(1, 5):
        total = total + blocks[:, column] * vector[column][None]
    return total

def from_next(values, axis, offset):
    length = values.shape[axis]
    shifted = lax.slice_in_dim(values, offset, length, axis=axis)
    padding = jnp.zeros_like(lax.slice_in_dim(values, 0, offset, axis=axis))
    return jnp.concatenate([shifted, padding], axis=axis)

def from_prior(values, axis, offset):
    length = values.shape[axis]
    shifted = lax.slice_in_dim(values, 0, length - offset, axis=axis)
    padding = jnp.zeros_like(lax.slice_in_dim(values, 0, offset, axis=axis))
    return jnp.concatenate([padding, shifted], axis=axis)

def place_faces(lower_term, upper_term, count, axis):
    if count == 1:
        return jnp.expand_dims(lower_term + upper_term, axis)
    lower_part = jnp.expand_dims(lower_term, axis)
    middle_part = jnp.repeat(jnp.zeros_like(lower_part), count - 2, axis=axis)
    return jnp.concatenate([lower_part, middle_part, jnp.expand_dims(upper_term, axis)], axis=axis)

def face_terms(values, penalty):
    count = values.shape[1]
    lanes = values.shape[-1]
    z_index = lax.broadcasted_iota(jnp.int32, (1, lanes), 1) % EZ
    has_next = (z_index < EZ - 1).astype(jnp.float32)
    has_prior = (z_index > 0).astype(jnp.float32)
    total = jnp.zeros_like(values)
    for direction in range(3):
        axis = direction + 1
        lower_face = jnp.take(values, 0, axis=axis)
        upper_face = jnp.take(values, count - 1, axis=axis)
        if direction == 0:
            next_lower = from_next(lower_face, 4, EZ)
            prior_upper = from_prior(upper_face, 4, EZ)
        elif direction == 1:
            next_lower = from_next(lower_face, 3, 1)
            prior_upper = from_prior(upper_face, 3, 1)
        else:
            next_lower = from_next(lower_face, 4, 1) * has_next
            prior_upper = from_prior(upper_face, 4, 1) * has_prior
        weight = penalty[direction]
        total = total + place_faces(weight * (lower_face - prior_upper), weight * (upper_face - next_lower), count, axis)
    return total

def apply_operator(values, flux_jacobian, time_term, penalty, derivative):
    result = time_term * values
    if derivative is not None:
        for direction in range(3):
            slopes = along_axis(derivative, values, direction + 1)
            result = result + block_product(flux_jacobian[direction][:, :, None, None, None], slopes)
    return result + face_terms(values, penalty)

def pre_smooth(source, blocks, operator):
    guess = DAMPING * block_product(blocks, source)
    return guess + DAMPING * block_product(blocks, source - operator(guess))

def post_smooth(source, guess, blocks, operator):
    for sweep_index in range(2):
        guess = guess + DAMPING * block_product(blocks, source - operator(guess))
    return guess

def reference(defect, point_inverse, flux_jacobian, time_term, penalty, element_inverse):
    derivative, coarse_derivative, interpolate = node_tables()
    rows = defect.shape[2]
    lanes = defect.shape[3]
    fine_blocks = point_inverse.reshape(5, 5, 4, 4, 4, rows, lanes)
    coarse_blocks = element_inverse[:, :, None, None, None]
    fine_source = defect.reshape(5, 4, 4, 4, rows, lanes)

    def fine_operator(values):
        return apply_operator(values, flux_jacobian, time_term, penalty, derivative)

    def middle_operator(values):
        return apply_operator(values, flux_jacobian, time_term, penalty, coarse_derivative)

    def bottom_operator(values):
        return apply_operator(values, flux_jacobian, time_term, penalty, None)
    fine_guess = pre_smooth(fine_source, fine_blocks, fine_operator)
    middle_source = three_axes(interpolate.T, fine_source - fine_operator(fine_guess))
    middle_guess = pre_smooth(middle_source, coarse_blocks, middle_operator)
    bottom_source = three_axes(np.ones((1, 2)), middle_source - middle_operator(middle_guess))
    bottom_guess = pre_smooth(bottom_source, coarse_blocks, bottom_operator)
    middle_guess = middle_guess + three_axes(np.ones((2, 1)), bottom_guess)
    middle_guess = post_smooth(middle_source, middle_guess, coarse_blocks, middle_operator)
    fine_guess = fine_guess + three_axes(interpolate, middle_guess)
    fine_guess = post_smooth(fine_source, fine_guess, fine_blocks, fine_operator)
    return fine_guess.reshape(5, 64, rows, lanes)
```

```python
import jax
import jax.numpy as jnp
import numpy as np
from jax import lax
from jax.experimental import pallas as pl
from jax.experimental.pallas import tpu as pltpu
from jax.sharding import PartitionSpec as P

EZ = 32
DAMPING = 0.7
MESH = pl.DeviceIdType.MESH
F32 = jnp.float32

STEPS = ((1, 0), (-1, 0), (0, 1), (0, -1), (1, 1), (1, -1), (-1, 1), (-1, -1))
RIGHT, LEFT, UP, DOWN, RIGHT_UP, RIGHT_DOWN, LEFT_UP, LEFT_DOWN = range(8)


def node_tables():
    points = np.array([-1.0, -1.0 / np.sqrt(5.0), 1.0 / np.sqrt(5.0), 1.0])
    barycentric = np.array(
        [1.0 / np.prod([points[j] - points[k] for k in range(4) if k != j]) for j in range(4)]
    )
    derivative = np.zeros((4, 4))
    for i in range(4):
        for j in range(4):
            if i != j:
                derivative[i, j] = barycentric[j] / barycentric[i] / (points[i] - points[j])
        derivative[i, i] = -np.sum(derivative[i])
    return derivative, (1.0 - points[1]) / 2.0, (1.0 + points[1]) / 2.0


DERIVATIVE, NEAR, FAR = node_tables()
EVEN = [float((DERIVATIVE[i, 0] + DERIVATIVE[i, 3]) / 2.0) for i in (0, 1)]
ODD = [[float((DERIVATIVE[i, j] - DERIVATIVE[i, 3 - j]) / 2.0) for j in (0, 1)] for i in (0, 1)]
NEAR, FAR = float(NEAR), float(FAR)


def roll_lanes(value, shift):
    shift %= 128
    return value if shift == 0 else pltpu.roll(value, shift, value.ndim - 1)


def roll_rows(value, shift):
    shift %= 8
    return value if shift == 0 else pltpu.roll(value, shift, value.ndim - 2)


def line_slopes(u0, u1, u2, u3):
    outer, inner = u0 - u3, u1 - u2
    even = (u0 + u3) - (u1 + u2)
    e0, e1 = EVEN[0] * even, EVEN[1] * even
    o0 = ODD[0][0] * outer + ODD[0][1] * inner
    o1 = ODD[1][0] * outer + ODD[1][1] * inner
    return o0 + e0, o1 + e1, o1 - e1, o0 - e0


def kernel(
    sec_count, dom_count,
    s_ref, b_ref, j_ref, t_ref, p_ref, e_ref,
    x_ref,
    jd, own, dg, res, sly, slz,
    fsend, frecv, ssend, srecv, esend, erecv, dsend, drecv, dssend, dsrecv,
    wst, wm, ws, wres, wsl, wc, wrx, wry, wb, fin,
    f_ss, f_rs, s_ss, s_rs, e_ss, e_rs,
):
    me_sec, me_dom = lax.axis_index("sec"), lax.axis_index("dom")
    has_dom = {0: None, 1: me_dom < dom_count - 1, -1: me_dom > 0}
    has_sec = {0: None, 1: me_sec < sec_count - 1, -1: me_sec > 0}

    def exists(dx, dy):
        a, b = has_dom[dx], has_sec[dy]
        if a is None:
            return b
        if b is None:
            return a
        return jnp.logical_and(a, b)

    def target(direction):
        dx, dy = STEPS[direction]
        return (me_sec + dy, me_dom + dx)

    barrier = pltpu.get_barrier_semaphore()
    for direction in range(8):
        @pl.when(exists(*STEPS[direction]))
        def _(direction=direction):
            pl.semaphore_signal(barrier, inc=1, device_id=target(direction), device_id_type=MESH)
    one, zero = jnp.int32(1), jnp.int32(0)
    across = jnp.where(me_dom < dom_count - 1, one, zero) + jnp.where(me_dom > 0, one, zero) + 1
    along = jnp.where(me_sec < sec_count - 1, one, zero) + jnp.where(me_sec > 0, one, zero) + 1

    def copy(direction, src, dst, send_sem, recv_sem):
        return pltpu.make_async_remote_copy(
            src_ref=src, dst_ref=dst, send_sem=send_sem, recv_sem=recv_sem,
            device_id=target(direction), device_id_type=MESH,
        )

    def send(direction, src, dst, send_sem, recv_sem):
        @pl.when(exists(*STEPS[direction]))
        def _():
            copy(direction, src, dst, send_sem, recv_sem).start()

    def sent(direction, src, dst, send_sem, recv_sem):
        @pl.when(exists(*STEPS[direction]))
        def _():
            copy(direction, src, dst, send_sem, recv_sem).wait_send()

    def arrived(direction, src, dst, send_sem, recv_sem):
        dx, dy = STEPS[direction]

        @pl.when(exists(-dx, -dy))
        def _():
            copy(direction, src, dst, send_sem, recv_sem).wait_recv()

    def clear(direction, dst):
        dx, dy = STEPS[direction]

        @pl.when(jnp.logical_not(exists(-dx, -dy)))
        def _():
            dst[...] = jnp.zeros_like(dst)

    def fine_message(stage, direction):
        return (direction, fsend.at[stage, direction], frecv.at[stage, direction],
                f_ss.at[stage, direction], f_rs.at[stage, direction])

    def static_message(direction):
        if direction < 4:
            src, dst = ssend.at[direction], srecv.at[direction]
        else:
            src, dst = dssend.at[direction - 4], dsrecv.at[direction - 4]
        return direction, src, dst, s_ss.at[direction], s_rs.at[direction]

    def coarse_message(stage, direction):
        if direction < 4:
            src, dst = esend.at[stage, direction], erecv.at[stage, direction]
        else:
            src, dst = dsend.at[stage, direction - 4], drecv.at[stage, direction - 4]
        return direction, src, dst, e_ss.at[stage, direction], e_rs.at[stage, direction]

    lane = lax.broadcasted_iota(jnp.int32, (8, 128), 1)
    row = lax.broadcasted_iota(jnp.int32, (8, 128), 0)
    low_half = row < 4
    low_lanes = lane < 64
    z_index = lane % EZ
    has_next = jnp.where(z_index < EZ - 1, 1.0, 0.0)
    has_prior = jnp.where(z_index > 0, 1.0, 0.0)
    lower = jnp.where(low_half, 1.0, 0.0)
    upper = 1.0 - lower

    def halves(a, b):
        return jnp.where(low_half, F32(a), F32(b))

    for array, start, count, scale in ((j_ref, 0, 75, 0.5), (e_ref, 75, 25, DAMPING)):
        def spread(n, c, array=array, start=start, scale=scale):
            value = array[n]
            jd[start + n, 0:4] = value
            jd[start + n, 4:8] = value
            own[start + n] = scale * jd[start + n]
            return c
        lax.fori_loop(0, count, spread, 0)
    for n, value in enumerate((t_ref[...], p_ref[0], p_ref[1], p_ref[2])):
        own[100 + n, 0:4] = value
        own[100 + n, 4:8] = value
    time, pen_x, pen_y, pen_z = own[100], own[101], own[102], own[103]
    for f in range(2):
        for q in range(8):
            j, k2 = q // 2, q % 2
            total = time + pen_z * (lower if k2 == 0 else upper)
            if j in (0, 3):
                total = total + pen_y
            dg[f, q] = total + pen_x if f else total

    px_prior = jnp.where(lane >= EZ, pen_x, 0.0)
    px_next = jnp.where(lane < 128 - EZ, pen_x, 0.0)
    px_left = jnp.where(lane < EZ, pen_x, 0.0)
    px_right = jnp.where(lane >= 128 - EZ, pen_x, 0.0)
    row4 = row % 4
    py_prior = jnp.where(row4 != 0, pen_y, 0.0)
    py_next = jnp.where(row4 != 3, pen_y, 0.0)
    py_below = jnp.where(row4 == 0, pen_y, 0.0)
    py_above = jnp.where(row4 == 3, pen_y, 0.0)
    pz_prior = pen_z * lower * has_prior
    pz_next = pen_z * upper * has_next

    def smooth(source, first):
        def block(q, c):
            values = [source[a, :, q] for a in range(5)]
            for a in range(5):
                total = b_ref[a, 0, :, q] * values[0]
                for b in range(1, 5):
                    total = total + b_ref[a, b, :, q] * values[b]
                total = DAMPING * total
                x_ref[a, :, q] = total if first else x_ref[a, :, q] + total
            return c
        lax.fori_loop(0, 8, block, 0)

    def send_faces(stage):
        def pieces(face, rolled, place):
            packed = None
            for m in range(4):
                piece = rolled(face(m), m)
                packed = piece if packed is None else jnp.where(place == m, piece, packed)
            return packed

        def one_variable(a, c):
            fsend[stage, RIGHT, a] = pieces(
                lambda m: x_ref[a, 3, 2 * m:2 * m + 2], lambda v, m: roll_lanes(v, EZ * (m + 1)), lane // EZ)
            fsend[stage, LEFT, a] = pieces(
                lambda m: x_ref[a, 0, 2 * m:2 * m + 2], lambda v, m: roll_lanes(v, EZ * m), lane // EZ)
            fsend[stage, UP, a] = pieces(
                lambda m: x_ref[a, m, 6:8], lambda v, m: roll_rows(v, m - 3), row4)
            fsend[stage, DOWN, a] = pieces(
                lambda m: x_ref[a, m, 0:2], lambda v, m: roll_rows(v, m), row4)
            return c
        lax.fori_loop(0, 5, one_variable, 0)
        for direction in range(4):
            send(*fine_message(stage, direction))

    even_z = halves(EVEN[0], -EVEN[1])
    even_z_swapped = halves(EVEN[1], -EVEN[0])
    odd_z = halves(ODD[0][0], ODD[1][1])
    odd_z_cross = halves(ODD[0][1], ODD[1][0])
    odd_z_swapped = halves(ODD[1][1], ODD[0][0])
    odd_z_cross_swapped = halves(ODD[1][0], ODD[0][1])

    def residual():
        def slab(n, c):
            a, i = n // 4, n % 4
            face = 1 - ((i + 1) // 2) % 2
            u = x_ref[a, i]
            r = s_ref[a, i] - dg[face] * u
            pairs = u.reshape(4, 2, 8, 128)
            v0, v1 = pairs[:, 0], pairs[:, 1]
            w0, w1 = roll_rows(v0, 4), roll_rows(v1, 4)
            even = (v0 + w1) - (w0 + v1)
            outer, inner = v0 - w1, w0 - v1
            z0 = odd_z * outer + odd_z_cross * inner + even_z * even
            z1 = odd_z_swapped * inner + odd_z_cross_swapped * outer - even_z_swapped * even
            slz[a, i] = jnp.stack([z0, z1], axis=1).reshape(8, 8, 128)
            add0 = pz_prior * roll_lanes(w1, 1)
            add1 = pz_next * roll_lanes(w0, -1)
            r = r + jnp.stack([add0, add1], axis=1).reshape(8, 8, 128)
            y = line_slopes(u[0:2], u[2:4], u[4:6], u[6:8])
            sly[a, i] = jnp.concatenate(y, axis=0)
            first = r[0:2] + py_prior * roll_rows(u[6:8], 1)
            last = r[6:8] + py_next * roll_rows(u[0:2], -1)
            res[a, i] = jnp.concatenate([first, r[2:6], last], axis=0)
            return c
        lax.fori_loop(0, 20, slab, 0)

        def block(q, c):
            total, slopes = [], []
            for a in range(5):
                u = x_ref[a, :, q]
                r = res[a, :, q]
                first = r[0] + px_prior * roll_lanes(u[3], EZ)
                last = r[3] + px_next * roll_lanes(u[0], -EZ)
                total.append(jnp.stack([first, r[1], r[2], last]))
                slopes.append(jnp.stack(line_slopes(u[0], u[1], u[2], u[3])))
            for d in range(3):
                if d == 1:
                    slopes = [sly[a, :, q] for a in range(5)]
                if d == 2:
                    slopes = [slz[a, :, q] for a in range(5)]
                for a in range(5):
                    for b in range(5):
                        total[a] = total[a] - jd[d * 25 + a * 5 + b] * slopes[b]
            for a in range(5):
                res[a, :, q] = total[a]
            return c
        lax.fori_loop(0, 8, block, 0)

    def add_halo(stage):
        for direction in range(4):
            arrived(*fine_message(stage, direction))

        def one_variable(a, c):
            from_left, from_right = frecv[stage, RIGHT, a], frecv[stage, LEFT, a]
            from_below, from_above = frecv[stage, UP, a], frecv[stage, DOWN, a]
            for m in range(4):
                q = slice(2 * m, 2 * m + 2)
                res[a, 0, q] = res[a, 0, q] + px_left * roll_lanes(from_left, -EZ * m)
                res[a, 3, q] = res[a, 3, q] + px_right * roll_lanes(from_right, 128 - EZ * (m + 1))
            for m in range(4):
                res[a, m, 0:2] = res[a, m, 0:2] + py_below * roll_rows(from_below, -m)
                res[a, m, 6:8] = res[a, m, 6:8] + py_above * roll_rows(from_above, 3 - m)
            return c
        lax.fori_loop(0, 5, one_variable, 0)

    def pack_columns(value, first_block):
        quarter = value.shape[0] // 4
        packed = None
        for m in range(4):
            piece = roll_rows(roll_lanes(value[m * quarter:(m + 1) * quarter], 64 * (m % 2)), 4 * (m // 2))
            place = jnp.logical_and(row // 4 == m // 2, lane // 64 == (first_block + m) % 2)
            packed = piece if packed is None else jnp.where(place, piece, packed)
        return packed

    def pack_rows(value, first_pair):
        quarter = value.shape[0] // 4
        packed = None
        for m in range(4):
            piece = roll_rows(value[m * quarter:(m + 1) * quarter], 2 * m)
            packed = piece if packed is None else jnp.where(row // 2 == (first_pair + m) % 4, piece, packed)
        return packed

    def pack_corner(rows_packed, keep_low):
        half = rows_packed.shape[0] // 2
        return jnp.where(low_lanes == keep_low, rows_packed[:half], roll_lanes(rows_packed[half:], 64))

    def unpack_columns(from_right, from_left):
        out = []
        for m in range(4):
            both = jnp.where(lane // 64 == m % 2, from_right, from_left)
            out.append(roll_rows(roll_lanes(both, -64 * (m % 2)), -4 * (m // 2)))
        return out

    def unpack_rows(from_above, from_below):
        return [roll_rows(jnp.where(row // 2 == m, from_above, from_below), 4 - 2 * m) for m in range(4)]

    def unpack_corner(right, left):
        return jnp.concatenate(
            [jnp.where(low_lanes, right, left), roll_lanes(jnp.where(low_lanes, left, right), 64)], axis=0)

    def fill_window(window, mine, columns, rows, corners):
        quarter = mine.shape[0] // 4
        side = unpack_columns(columns[0], columns[1])
        ends = unpack_rows(rows[0], rows[1])
        above = unpack_corner(corners[0], corners[1])
        below = unpack_corner(corners[2], corners[3])
        edge = unpack_rows(above, below)
        for m in range(4):
            part = slice(m * quarter, (m + 1) * quarter)
            window[0, part] = jnp.where(low_half, mine[part], ends[m])
            window[1, part] = jnp.where(low_half, side[m], edge[m])

    smooth(s_ref, True)
    pl.semaphore_wait(barrier, across * along - 1)
    send_faces(0)

    coefficients = own[...]
    ssend[RIGHT] = pack_columns(coefficients, 1)
    ssend[LEFT] = pack_columns(coefficients, 0)
    ssend[UP] = pack_rows(coefficients, 1)
    ssend[DOWN] = pack_rows(coefficients, 0)
    for direction, source, keep_low in (
        (RIGHT_UP, UP, False), (RIGHT_DOWN, DOWN, False), (LEFT_UP, UP, True), (LEFT_DOWN, DOWN, True)
    ):
        dssend[direction - 4] = pack_corner(ssend[source], keep_low)
    for direction in range(8):
        send(*static_message(direction))
    for stage in range(3):
        for direction in range(4):
            clear(direction, frecv.at[stage, direction])
    for stage in range(2):
        for direction in range(4):
            clear(direction, erecv.at[stage, direction])
        for direction in range(4, 8):
            clear(direction, drecv.at[stage, direction - 4])
    for direction in range(4):
        clear(direction, srecv.at[direction])
    for direction in range(4, 8):
        clear(direction, dsrecv.at[direction - 4])

    residual()
    add_halo(0)
    smooth(res, False)
    send_faces(1)
    residual()
    for direction in range(8):
        arrived(*static_message(direction))
    fill_window(
        wst, own,
        (srecv[LEFT], srecv[RIGHT]), (srecv[DOWN], srecv[UP]),
        (dsrecv[LEFT_DOWN - 4], dsrecv[RIGHT_DOWN - 4], dsrecv[LEFT_UP - 4], dsrecv[RIGHT_UP - 4]),
    )
    add_halo(1)

    near_low, far_low = halves(1.0, NEAR), halves(FAR, 0.0)
    near_high, far_high = halves(NEAR, 1.0), halves(0.0, FAR)

    def restrict(a, c):
        for ip in range(2):
            if ip == 0:
                x = res[a, 0] + NEAR * res[a, 1] + FAR * res[a, 2]
            else:
                x = FAR * res[a, 1] + NEAR * res[a, 2] + res[a, 3]
            for jp in range(2):
                if jp == 0:
                    y = x[0:2] + NEAR * x[2:4] + FAR * x[4:6]
                else:
                    y = FAR * x[2:4] + NEAR * x[4:6] + x[6:8]
                z0 = near_low * y[0] + far_low * y[1]
                z1 = far_high * y[0] + near_high * y[1]
                n = a * 8 + ip * 4 + jp * 2
                fin[n] = z0 + roll_rows(z0, 4)
                fin[n + 1] = z1 + roll_rows(z1, 4)
        return c
    lax.fori_loop(0, 5, restrict, 0)

    def exchange(stage, field, faces):
        nodes = faces.reshape(5, 2, 2, 2, 8, 128)
        x_low, x_up = nodes[:, 0].reshape(20, 8, 128), nodes[:, 1].reshape(20, 8, 128)
        y_low, y_up = nodes[:, :, 0].reshape(20, 8, 128), nodes[:, :, 1].reshape(20, 8, 128)
        esend[stage, RIGHT, 0:10] = pack_columns(field, 1)
        esend[stage, RIGHT, 10:15] = pack_columns(roll_lanes(x_up, EZ), 1)
        esend[stage, LEFT, 0:10] = pack_columns(field, 0)
        esend[stage, LEFT, 10:15] = pack_columns(roll_lanes(x_low, -EZ), 0)
        esend[stage, UP, 0:10] = pack_rows(field, 1)
        esend[stage, UP, 10:15] = pack_rows(roll_rows(y_up, 1), 1)
        esend[stage, DOWN, 0:10] = pack_rows(field, 0)
        esend[stage, DOWN, 10:15] = pack_rows(roll_rows(y_low, -1), 0)
        for direction, source, keep_low in (
            (RIGHT_UP, UP, False), (RIGHT_DOWN, DOWN, False), (LEFT_UP, UP, True), (LEFT_DOWN, DOWN, True)
        ):
            dsend[stage, direction - 4] = pack_corner(esend[stage, source, 0:10], keep_low)
        for direction in (4, 5, 6, 7, 0, 1, 2, 3):
            send(*coarse_message(stage, direction))

    def receive(stage, window, field):
        for direction in range(8):
            arrived(*coarse_message(stage, direction))
        fill_window(
            window, field,
            (erecv[stage, LEFT, 0:10], erecv[stage, RIGHT, 0:10]),
            (erecv[stage, DOWN, 0:10], erecv[stage, UP, 0:10]),
            (drecv[stage, LEFT_DOWN - 4], drecv[stage, RIGHT_DOWN - 4],
             drecv[stage, LEFT_UP - 4], drecv[stage, RIGHT_UP - 4]),
        )
        side = unpack_columns(erecv[stage, LEFT, 10:15], erecv[stage, RIGHT, 10:15])
        ends = unpack_rows(erecv[stage, DOWN, 10:15], erecv[stage, UP, 10:15])
        for m in range(4):
            wrx[5 * m:5 * m + 5] = side[m]
            wry[5 * m:5 * m + 5] = ends[m]

    strip_right = jnp.logical_and(low_half, lane // EZ == 1)
    strip_left = jnp.logical_and(low_half, lane // EZ == 2)

    def across_x(low0, low1, up0, up1, strip):
        l0, l1 = roll_lanes(low0, -EZ), roll_lanes(low1, -EZ)
        u0, u1 = roll_lanes(up0, EZ), roll_lanes(up1, EZ)
        not_last, first = lane < 128 - EZ, lane < EZ
        next0, next1 = jnp.where(not_last, l0, l1), jnp.where(not_last, l1, l0)
        prior0, prior1 = jnp.where(first, u1, u0), jnp.where(first, u0, u1)
        if strip is not None:
            next1 = jnp.where(strip_right, strip, next1)
            prior1 = jnp.where(strip_left, strip, prior1)
        return (next0, next1), (prior0, prior1)

    def window_faces(a, use_strips):
        tiles = [wm[tile, pl.ds(a * 8, 8)] for tile in range(2)]
        nodes = [u.reshape(2, 2, 2, 8, 128) for u in tiles]
        x_low, x_up = [u[0].reshape(4, 8, 128) for u in nodes], [u[1].reshape(4, 8, 128) for u in nodes]
        y_low, y_up = [u[:, 0].reshape(4, 8, 128) for u in nodes], [u[:, 1].reshape(4, 8, 128) for u in nodes]
        z_low, z_up = [u[:, :, 0].reshape(4, 8, 128) for u in nodes], [u[:, :, 1].reshape(4, 8, 128) for u in nodes]
        x_next, x_prior = across_x(
            x_low[0], x_low[1], x_up[0], x_up[1], wrx[pl.ds(a * 4, 4)] if use_strips else None)
        out = []
        for tile in range(2):
            px, py, pz = wst[tile, 101], wst[tile, 102], wst[tile, 103]
            x = (px * (x_low[tile] - x_prior[tile]), px * (x_up[tile] - x_next[tile]))
            y_next, y_prior = roll_rows(y_low[tile], -1), roll_rows(y_up[tile], 1)
            if tile == 0 and use_strips:
                strip = wry[pl.ds(a * 4, 4)]
                y_next = jnp.where(row == 5, strip, y_next)
                y_prior = jnp.where(row == 6, strip, y_prior)
            y = (py * (y_low[tile] - y_prior), py * (y_up[tile] - y_next))
            z = (pz * (z_low[tile] - has_prior * roll_lanes(z_up[tile], 1)),
                 pz * (z_up[tile] - has_next * roll_lanes(z_low[tile], -1)))
            slopes = (x_up[tile] - x_low[tile], y_up[tile] - y_low[tile], z_up[tile] - z_low[tile])
            out.append((tiles[tile], x, y, z, slopes))
        return out

    def fluxes(tiles):
        def one(n, c):
            d, tile = n // tiles, n % tiles
            slopes = [wsl[tile, d, b] for b in range(5)]
            for a in range(5):
                total = wst[tile, d * 25 + a * 5] * slopes[0]
                for b in range(1, 5):
                    total = total + wst[tile, d * 25 + a * 5 + b] * slopes[b]
                wc[tile, d, a] = total
            return c
        lax.fori_loop(0, 3 * tiles, one, 0)

    def middle_residual(use_strips):
        def one(a, c):
            for tile, (u, x, y, z, slopes) in enumerate(window_faces(a, use_strips)):
                r = ws[tile, pl.ds(a * 8, 8)] - wst[tile, 100] * u
                r = r.reshape(2, 2, 2, 8, 128)
                r = r - jnp.stack(x, axis=0).reshape(2, 2, 2, 8, 128)
                r = r - jnp.stack([v.reshape(2, 2, 8, 128) for v in y], axis=1)
                r = r - jnp.stack([v.reshape(2, 2, 8, 128) for v in z], axis=2)
                wres[tile, a] = r.reshape(8, 8, 128)
                for d in range(3):
                    wsl[tile, d, a] = slopes[d]
            return c
        lax.fori_loop(0, 5, one, 0)
        fluxes(2)

    def full_residual(tile, ip, a):
        r = wres[tile, a, pl.ds(ip * 4, 4)].reshape(2, 2, 8, 128)
        r = r - wc[tile, 0, a].reshape(2, 2, 8, 128)
        r = r - wc[tile, 1, a, pl.ds(ip * 2, 2)][None]
        return r - wc[tile, 2, a, pl.ds(ip * 2, 2)][:, None]

    def middle_sweep(use_strips):
        middle_residual(use_strips)

        def one(n, c):
            tile, ip = n // 2, n % 2
            r = [full_residual(tile, ip, a).reshape(4, 8, 128) for a in range(5)]
            for a in range(5):
                part = pl.ds(a * 8 + ip * 4, 4)
                total = wm[tile, part]
                for b in range(5):
                    total = total + wst[tile, 75 + a * 5 + b] * r[b]
                wm[tile, part] = total
            return c
        lax.fori_loop(0, 4, one, 0)

    def element_product(tile, values):
        out = []
        for a in range(5):
            total = wst[tile, 75 + a * 5] * values[0]
            for b in range(1, 5):
                total = total + wst[tile, 75 + a * 5 + b] * values[b]
            out.append(total)
        return out

    def own_guess(n, c):
        part = [fin[pl.ds(b * 8 + n * 4, 4)] for b in range(5)]
        for a, value in enumerate(element_product(0, part)):
            fin[pl.ds(40 + a * 8 + n * 4, 4)] = value
        return c
    lax.fori_loop(0, 2, own_guess, 0)
    exchange(0, fin[0:40], fin[40:80])
    receive(0, ws, fin[0:40])

    def first_guess(n, c):
        tile, ip = n // 2, n % 2
        part = [ws[tile, pl.ds(b * 8 + ip * 4, 4)] for b in range(5)]
        for a, value in enumerate(element_product(tile, part)):
            wm[tile, pl.ds(a * 8 + ip * 4, 4)] = value
        return c
    lax.fori_loop(0, 4, first_guess, 0)
    middle_sweep(True)
    middle_residual(False)

    for tile in range(2):
        def bottom_source(a, c, tile=tile):
            total = full_residual(tile, 0, a) + full_residual(tile, 1, a)
            total = total[0] + total[1]
            wb[0, tile, a] = total[0] + total[1]
            return c
        lax.fori_loop(0, 5, bottom_source, 0)
    for tile in range(2):
        values = [wb[0, tile, a] for a in range(5)]
        for a, value in enumerate(element_product(tile, values)):
            wb[1, tile, a] = value
    bottom = wb[1, 0]
    (x_next, _), (x_prior, _) = across_x(bottom, wb[1, 1], bottom, wb[1, 1], None)
    applied = (time + 2.0 * (pen_x + pen_y + pen_z)) * bottom
    applied = applied - pen_x * (x_next + x_prior)
    applied = applied - pen_y * (roll_rows(bottom, 1) + roll_rows(bottom, -1))
    applied = applied - pen_z * (has_prior * roll_lanes(bottom, 1) + has_next * roll_lanes(bottom, -1))
    rest = wb[0, 0] - applied
    change = element_product(0, [rest[b] for b in range(5)])
    for a in range(5):
        fin[a * 8:a * 8 + 8] = wm[0, a * 8:a * 8 + 8] + (bottom[a] + change[a])

    exchange(1, fin[0:40], fin[0:40])
    receive(1, wm, fin[0:40])
    middle_sweep(True)
    middle_sweep(False)

    def final_parts(a, c):
        u, x, y, z, slopes = window_faces(a, False)[0]
        for d in range(3):
            wsl[0, d, a] = slopes[d]
        wres[0, a] = wst[0, 100] * u
        for d, terms in enumerate((x, y, z)):
            for side in range(2):
                fin[pl.ds((d * 2 + side) * 20 + a * 4, 4)] = terms[side]
        return c
    lax.fori_loop(0, 5, final_parts, 0)
    fluxes(1)

    def both(value):
        return jnp.where(low_half, value, roll_rows(value, 4))

    low_a, low_b = halves(1.0, NEAR), halves(0.0, FAR)
    high_a, high_b = halves(FAR, 0.0), halves(NEAR, 1.0)

    def spread_z(v0, v1):
        return low_a * v0 + low_b * v1, high_a * v0 + high_b * v1

    def spread_line(v0, v1):
        return v0, NEAR * v0 + FAR * v1, FAR * v0 + NEAR * v1, v1

    def prolong(value):
        value = both(value)
        z0, z1 = spread_z(value[:, :, 0], value[:, :, 1])
        pairs = jnp.stack([z0, z1], axis=2)
        lines = jnp.concatenate([v for v in spread_line(pairs[:, 0], pairs[:, 1])], axis=1)
        return spread_line(lines[0], lines[1])

    def final_fine(a, c):
        for i, value in enumerate(prolong(wm[0, pl.ds(a * 8, 8)].reshape(2, 2, 2, 8, 128))):
            x_ref[a, i] = x_ref[a, i] + value
        volume = wres[0, a].reshape(2, 2, 2, 8, 128) + wc[0, 0, a].reshape(1, 2, 2, 8, 128)
        volume = volume + wc[0, 1, a].reshape(2, 1, 2, 8, 128) + wc[0, 2, a].reshape(2, 2, 1, 8, 128)
        for i, value in enumerate(prolong(volume)):
            res[a, i] = res[a, i] - value
        for side in range(2):
            i, j, k2 = 3 * side, slice(6 * side, 6 * side + 2), side
            face = both(fin[pl.ds(side * 20 + a * 4, 4)].reshape(2, 2, 8, 128))
            z = jnp.stack(spread_z(face[:, 0], face[:, 1]), axis=1)
            res[a, i] = res[a, i] - jnp.concatenate(spread_line(z[0], z[1]), axis=0)
            face = both(fin[pl.ds((2 + side) * 20 + a * 4, 4)].reshape(2, 2, 8, 128))
            z = jnp.stack(spread_z(face[:, 0], face[:, 1]), axis=1)
            for m, value in enumerate(spread_line(z[0], z[1])):
                res[a, m, j] = res[a, m, j] - value
            face = fin[pl.ds((4 + side) * 20 + a * 4, 4)].reshape(2, 2, 8, 128)
            face = lower * face if side == 0 else upper * roll_rows(face, 4)
            lines = jnp.stack(spread_line(face[:, 0], face[:, 1]), axis=1)
            for m, value in enumerate(spread_line(lines[0], lines[1])):
                for n in range(4):
                    res[a, m, 2 * n + k2] = res[a, m, 2 * n + k2] - value[n]
        return c
    lax.fori_loop(0, 5, final_fine, 0)
    smooth(res, False)

    send_faces(2)
    residual()
    add_halo(2)
    smooth(res, False)

    for stage in range(3):
        for direction in range(4):
            sent(*fine_message(stage, direction))
    for direction in range(8):
        sent(*static_message(direction))
    for stage in range(2):
        for direction in range(8):
            sent(*coarse_message(stage, direction))


def solution(mesh):
    sec_count, dom_count = mesh.shape["sec"], mesh.shape["dom"]

    def on_device(defect, point_inverse, flux_jacobian, time_term, penalty, element_inverse):
        def run(*refs):
            kernel(sec_count, dom_count, *refs)

        vmem = lambda *shape: pltpu.VMEM(shape + (8, 128), F32)
        dma = lambda *shape: pltpu.SemaphoreType.DMA(shape)
        out = pl.pallas_call(
            run,
            out_shape=jax.ShapeDtypeStruct((5, 4, 8, 8, 128), F32),
            in_specs=[pl.BlockSpec(memory_space=pltpu.VMEM)] * 6,
            out_specs=pl.BlockSpec(memory_space=pltpu.VMEM),
            scratch_shapes=[
                vmem(100), vmem(104), vmem(2, 8), vmem(5, 4, 8), vmem(5, 4, 8), vmem(5, 4, 8),
                vmem(3, 4, 5, 2), vmem(3, 4, 5, 2), vmem(4, 26), vmem(4, 26),
                vmem(2, 4, 15), vmem(2, 4, 15), vmem(2, 4, 5), vmem(2, 4, 5), vmem(4, 13), vmem(4, 13),
                vmem(2, 104), vmem(2, 40), vmem(2, 40), vmem(2, 5, 8), vmem(2, 3, 5, 4), vmem(2, 3, 5, 4),
                vmem(20), vmem(20), vmem(2, 2, 5), vmem(120),
                dma(3, 4), dma(3, 4), dma(8), dma(8), dma(2, 8), dma(2, 8),
            ],
            compiler_params=pltpu.CompilerParams(
                collective_id=0, has_side_effects=True, vmem_limit_bytes=48 << 20
            ),
        )(
            defect.reshape(5, 4, 8, 8, 128),
            point_inverse.reshape(5, 5, 4, 8, 8, 128),
            flux_jacobian.reshape(75, 4, 128),
            time_term,
            penalty,
            element_inverse.reshape(25, 4, 128),
        )
        return out.reshape(5, 64, 4, 128)

    placed = (
        P(None, None, "sec", "dom"),
        P(None, None, None, "sec", "dom"),
        P(None, None, None, "sec", "dom"),
        P("sec", "dom"),
        P(None, "sec", "dom"),
        P(None, None, "sec", "dom"),
    )
    return jax.shard_map(
        on_device,
        mesh=mesh,
        in_specs=placed,
        out_specs=P(None, None, "sec", "dom"),
        check_vma=False,
    )
```

```python
import jax
import jax.numpy as jnp
import numpy as np
from jax import lax
from jax.experimental import pallas as pl
from jax.experimental.pallas import tpu as pltpu
from jax.sharding import PartitionSpec as P

EZ = 32
DAMPING = 0.7
MESH = pl.DeviceIdType.MESH
F32 = jnp.float32

STEPS = ((1, 0), (-1, 0), (0, 1), (0, -1), (1, 1), (1, -1), (-1, 1), (-1, -1))
RIGHT, LEFT, UP, DOWN, RIGHT_UP, RIGHT_DOWN, LEFT_UP, LEFT_DOWN = range(8)


def node_tables():
    points = np.array([-1.0, -1.0 / np.sqrt(5.0), 1.0 / np.sqrt(5.0), 1.0])
    barycentric = np.array(
        [1.0 / np.prod([points[j] - points[k] for k in range(4) if k != j]) for j in range(4)]
    )
    derivative = np.zeros((4, 4))
    for i in range(4):
        for j in range(4):
            if i != j:
                derivative[i, j] = barycentric[j] / barycentric[i] / (points[i] - points[j])
        derivative[i, i] = -np.sum(derivative[i])
    return derivative, (1.0 - points[1]) / 2.0, (1.0 + points[1]) / 2.0


DERIVATIVE, NEAR, FAR = node_tables()
EVEN = [float((DERIVATIVE[i, 0] + DERIVATIVE[i, 3]) / 2.0) for i in (0, 1)]
ODD = [[float((DERIVATIVE[i, j] - DERIVATIVE[i, 3 - j]) / 2.0) for j in (0, 1)] for i in (0, 1)]
NEAR, FAR = float(NEAR), float(FAR)


def roll_lanes(value, shift):
    shift %= 128
    return value if shift == 0 else pltpu.roll(value, shift, value.ndim - 1)


def roll_rows(value, shift):
    shift %= 8
    return value if shift == 0 else pltpu.roll(value, shift, value.ndim - 2)


def kernel(
    sec_count, dom_count,
    s_hbm, b_hbm, j_hbm, t_hbm, p_hbm, e_hbm,
    out_ref,
    s_ref, b_ref, j_ref, t_ref, p_ref, e_ref,
    x_ref, jd, own, dg, res,
    fsend, frecv, ssend, srecv, esend, erecv, dsend, drecv, dssend, dsrecv,
    wst, wm, ws, wres, wsl, wc, wrx, wry, wb, fin,
    f_ss, f_rs, s_ss, s_rs, e_ss, e_rs, in_sem,
):
    small = [
        pltpu.make_async_copy(source, kept, in_sem.at[4 + n])
        for n, (source, kept) in enumerate(
            ((s_hbm, s_ref), (j_hbm, j_ref), (e_hbm, e_ref), (t_hbm, t_ref), (p_hbm, p_ref)))
    ]
    blocks = [
        pltpu.make_async_copy(b_hbm.at[:, :, i], b_ref.at[:, :, i], in_sem.at[i]) for i in range(4)
    ]
    for transfer in small + blocks:
        transfer.start()
    me_sec, me_dom = lax.axis_index("sec"), lax.axis_index("dom")
    has_dom = {0: None, 1: me_dom < dom_count - 1, -1: me_dom > 0}
    has_sec = {0: None, 1: me_sec < sec_count - 1, -1: me_sec > 0}

    def exists(dx, dy):
        a, b = has_dom[dx], has_sec[dy]
        if a is None:
            return b
        if b is None:
            return a
        return jnp.logical_and(a, b)

    def target(direction):
        dx, dy = STEPS[direction]
        return (me_sec + dy, me_dom + dx)

    barrier = pltpu.get_barrier_semaphore()
    for direction in range(8):
        @pl.when(exists(*STEPS[direction]))
        def _(direction=direction):
            pl.semaphore_signal(barrier, inc=1, device_id=target(direction), device_id_type=MESH)
    one, zero = jnp.int32(1), jnp.int32(0)
    across = jnp.where(me_dom < dom_count - 1, one, zero) + jnp.where(me_dom > 0, one, zero) + 1
    along = jnp.where(me_sec < sec_count - 1, one, zero) + jnp.where(me_sec > 0, one, zero) + 1

    def copy(direction, src, dst, send_sem, recv_sem):
        return pltpu.make_async_remote_copy(
            src_ref=src, dst_ref=dst, send_sem=send_sem, recv_sem=recv_sem,
            device_id=target(direction), device_id_type=MESH,
        )

    def send(direction, src, dst, send_sem, recv_sem):
        @pl.when(exists(*STEPS[direction]))
        def _():
            copy(direction, src, dst, send_sem, recv_sem).start()

    def sent(direction, src, dst, send_sem, recv_sem):
        @pl.when(exists(*STEPS[direction]))
        def _():
            copy(direction, src, dst, send_sem, recv_sem).wait_send()

    def arrived(direction, src, dst, send_sem, recv_sem):
        dx, dy = STEPS[direction]

        @pl.when(exists(-dx, -dy))
        def _():
            copy(direction, src, dst, send_sem, recv_sem).wait_recv()

    def clear(direction, dst):
        dx, dy = STEPS[direction]

        @pl.when(jnp.logical_not(exists(-dx, -dy)))
        def _():
            dst[...] = jnp.zeros_like(dst)

    def fine_message(stage, direction):
        return (direction, fsend.at[stage, direction], frecv.at[stage, direction],
                f_ss.at[stage, direction], f_rs.at[stage, direction])

    def static_message(direction):
        if direction < 4:
            src, dst = ssend.at[direction], srecv.at[direction]
        else:
            src, dst = dssend.at[direction - 4], dsrecv.at[direction - 4]
        return direction, src, dst, s_ss.at[direction], s_rs.at[direction]

    def coarse_message(stage, direction):
        if direction < 4:
            src, dst = esend.at[stage, direction], erecv.at[stage, direction]
        else:
            src, dst = dsend.at[stage, direction - 4], drecv.at[stage, direction - 4]
        return direction, src, dst, e_ss.at[stage, direction], e_rs.at[stage, direction]

    lane = lax.broadcasted_iota(jnp.int32, (8, 128), 1)
    row = lax.broadcasted_iota(jnp.int32, (8, 128), 0)
    low_half = row < 4
    low_lanes = lane < 64
    z_index = lane % EZ
    has_next = jnp.where(z_index < EZ - 1, 1.0, 0.0)
    has_prior = jnp.where(z_index > 0, 1.0, 0.0)
    lower = jnp.where(low_half, 1.0, 0.0)
    upper = 1.0 - lower

    def halves(a, b):
        return jnp.where(low_half, F32(a), F32(b))

    for transfer in small[1:]:
        transfer.wait()
    for array, start, count, scale in ((j_ref, 0, 75, 0.5), (e_ref, 75, 25, DAMPING)):
        value = array[...]
        jd[start:start + count, 0:4] = value
        jd[start:start + count, 4:8] = value
    own[0:75] = 0.5 * jd[0:75]
    own[75:100] = DAMPING * jd[75:100]
    for n, value in enumerate((t_ref[...], p_ref[0], p_ref[1], p_ref[2])):
        own[100 + n, 0:4] = value
        own[100 + n, 4:8] = value
    time, pen_x, pen_y, pen_z = own[100], own[101], own[102], own[103]
    for f in range(2):
        for j in range(4):
            for k2 in range(2):
                total = time + pen_z * (lower if k2 == 0 else upper)
                if j in (0, 3):
                    total = total + pen_y
                dg[f, j, k2] = total + pen_x if f else total

    px_prior = jnp.where(lane >= EZ, pen_x, 0.0)
    px_next = jnp.where(lane < 128 - EZ, pen_x, 0.0)
    px_left = jnp.where(lane < EZ, pen_x, 0.0)
    px_right = jnp.where(lane >= 128 - EZ, pen_x, 0.0)
    row4 = row % 4
    py_prior = jnp.where(row4 != 0, pen_y, 0.0)
    py_next = jnp.where(row4 != 3, pen_y, 0.0)
    py_below = jnp.where(row4 == 0, pen_y, 0.0)
    py_above = jnp.where(row4 == 3, pen_y, 0.0)
    pz_prior = pen_z * lower * has_prior
    pz_next = pen_z * upper * has_next

    def smooth(source, i, j, target, first):
        part = pl.ds(j, 2)
        values = [source[a, i, part] for a in range(5)]
        totals = []
        for a in range(5):
            total = b_ref[a, 0, i, part] * values[0]
            for b in range(1, 5):
                total = total + b_ref[a, b, i, part] * values[b]
            total = DAMPING * total
            totals.append(total if first else x_ref[a, i, part] + total)
        for a in range(5):
            target[a, i, part] = totals[a]

    def smooth_all(target):
        def block(n, c):
            smooth(res, n // 2, 2 * (n % 2), target, False)
            return c
        lax.fori_loop(0, 8, block, 0)

    def send_faces(stage):
        def pieces(face, rolled, place):
            packed = None
            for m in range(4):
                piece = rolled(face(m), m)
                packed = piece if packed is None else jnp.where(place == m, piece, packed)
            return packed

        fsend[stage, RIGHT] = pieces(
            lambda m: x_ref[:, 3, m], lambda v, m: roll_lanes(v, EZ * (m + 1)), lane // EZ)
        fsend[stage, LEFT] = pieces(
            lambda m: x_ref[:, 0, m], lambda v, m: roll_lanes(v, EZ * m), lane // EZ)
        for direction in (RIGHT, LEFT):
            send(*fine_message(stage, direction))
        fsend[stage, UP] = pieces(
            lambda m: x_ref[:, m, 3], lambda v, m: roll_rows(v, m - 3), row4)
        fsend[stage, DOWN] = pieces(
            lambda m: x_ref[:, m, 0], lambda v, m: roll_rows(v, m), row4)
        for direction in (UP, DOWN):
            send(*fine_message(stage, direction))

    even_z = halves(EVEN[0], EVEN[1])
    even_z_swapped = halves(EVEN[1], EVEN[0])
    odd_z = halves(ODD[0][0], ODD[1][1])
    odd_z_cross = halves(ODD[0][1], ODD[1][0])
    odd_z_swapped = halves(ODD[1][1], ODD[0][0])
    odd_z_cross_swapped = halves(ODD[1][0], ODD[0][1])

    def jacobian(d, parts):
        out = []
        for a in range(5):
            total = [jd[d * 25 + a * 5] * value for value in parts[0]]
            for b in range(1, 5):
                block = jd[d * 25 + a * 5 + b]
                total = [t + block * value for t, value in zip(total, parts[b])]
            out.append(total)
        return out

    def line_parts(u):
        return [u[0] - u[3], u[1] - u[2], (u[0] + u[3]) - (u[1] + u[2])]

    def line_slopes(outer, inner, even):
        e0, e1 = EVEN[0] * even, EVEN[1] * even
        o0 = ODD[0][0] * outer + ODD[0][1] * inner
        o1 = ODD[1][0] * outer + ODD[1][1] * inner
        return o0 + e0, o1 + e1, o1 - e1, o0 - e0

    def residual():
        def along_x(n, c):
            j, k2 = n // 2, n % 2
            inner_weight, outer_weight = dg[0, j, k2], dg[1, j, k2]
            u = [x_ref[a, :, j, k2] for a in range(5)]
            flux = jacobian(0, [line_parts(v) for v in u])
            out = []
            for a in range(5):
                slopes = line_slopes(*flux[a])
                s = s_ref[a, :, j, k2]
                v = u[a]
                out.append(jnp.stack([
                    (s[0] - outer_weight * v[0]) + (px_prior * roll_lanes(v[3], EZ) - slopes[0]),
                    (s[1] - inner_weight * v[1]) - slopes[1],
                    (s[2] - inner_weight * v[2]) - slopes[2],
                    (s[3] - outer_weight * v[3]) + (px_next * roll_lanes(v[0], -EZ) - slopes[3]),
                ]))
            for a in range(5):
                res[a, :, j, k2] = out[a]
            return c
        lax.fori_loop(0, 8, along_x, 0)

        def along_y(n, c):
            i, k2 = n // 2, n % 2
            u = [x_ref[a, i, :, k2] for a in range(5)]
            flux = jacobian(1, [line_parts(v) for v in u])
            out = []
            for a in range(5):
                slopes = line_slopes(*flux[a])
                r = res[a, i, :, k2]
                v = u[a]
                out.append(jnp.stack([
                    r[0] + (py_prior * roll_rows(v[3], 1) - slopes[0]),
                    r[1] - slopes[1],
                    r[2] - slopes[2],
                    r[3] + (py_next * roll_rows(v[0], -1) - slopes[3]),
                ]))
            for a in range(5):
                res[a, i, :, k2] = out[a]
            return c
        lax.fori_loop(0, 8, along_y, 0)

        def along_z(n, c):
            i, j = n // 2, 2 * (n % 2)
            part = pl.ds(j, 2)
            parts, adds = [], []
            for a in range(5):
                u = x_ref[a, i, part]
                v0, v1 = u[:, 0], u[:, 1]
                w0, w1 = roll_rows(v0, 4), roll_rows(v1, 4)
                straight, swapped = v0 + w1, w0 + v1
                odd = v0 - w1
                even = jnp.where(low_half, straight[0] - swapped[0], swapped[1] - straight[1])
                parts.append([odd[0], odd[1], even])
                adds.append(jnp.stack([pz_prior * roll_lanes(w1, 1), pz_next * roll_lanes(w0, -1)], axis=1))
            flux = jacobian(2, parts)
            out = []
            for a in range(5):
                turned = roll_rows(flux[a][2], 4)
                even = (jnp.where(low_half, flux[a][2], turned), jnp.where(low_half, turned, flux[a][2]))
                lines = []
                for m in range(2):
                    odd = flux[a][m]
                    cross = roll_rows(odd, 4)
                    lines.append(jnp.stack([
                        odd_z * odd + odd_z_cross * cross + even_z * even[m],
                        odd_z_swapped * cross + odd_z_cross_swapped * odd - even_z_swapped * even[m],
                    ]))
                out.append(res[a, i, part] + (adds[a] - jnp.stack(lines)))
            for a in range(5):
                res[a, i, part] = out[a]
            return c
        lax.fori_loop(0, 8, along_z, 0)

    def add_halo(stage):
        for direction in range(4):
            arrived(*fine_message(stage, direction))
        from_left, from_right = frecv[stage, RIGHT], frecv[stage, LEFT]
        from_below, from_above = frecv[stage, UP], frecv[stage, DOWN]
        for m in range(4):
            res[:, 0, m] = res[:, 0, m] + px_left * roll_lanes(from_left, -EZ * m)
            res[:, 3, m] = res[:, 3, m] + px_right * roll_lanes(from_right, 128 - EZ * (m + 1))
        for m in range(4):
            res[:, m, 0] = res[:, m, 0] + py_below * roll_rows(from_below, -m)
            res[:, m, 3] = res[:, m, 3] + py_above * roll_rows(from_above, 3 - m)

    def pack_columns(value, first_block):
        quarter = value.shape[0] // 4
        packed = None
        for m in range(4):
            piece = roll_rows(roll_lanes(value[m * quarter:(m + 1) * quarter], 64 * (m % 2)), 4 * (m // 2))
            place = jnp.logical_and(row // 4 == m // 2, lane // 64 == (first_block + m) % 2)
            packed = piece if packed is None else jnp.where(place, piece, packed)
        return packed

    def pack_rows(value, first_pair):
        quarter = value.shape[0] // 4
        packed = None
        for m in range(4):
            piece = roll_rows(value[m * quarter:(m + 1) * quarter], 2 * m)
            packed = piece if packed is None else jnp.where(row // 2 == (first_pair + m) % 4, piece, packed)
        return packed

    def pack_corner(rows_packed, keep_low):
        half = rows_packed.shape[0] // 2
        return jnp.where(low_lanes == keep_low, rows_packed[:half], roll_lanes(rows_packed[half:], 64))

    def unpack_columns(from_right, from_left):
        out = []
        for m in range(4):
            both = jnp.where(lane // 64 == m % 2, from_right, from_left)
            out.append(roll_rows(roll_lanes(both, -64 * (m % 2)), -4 * (m // 2)))
        return out

    def unpack_rows(from_above, from_below):
        return [roll_rows(jnp.where(row // 2 == m, from_above, from_below), 4 - 2 * m) for m in range(4)]

    def unpack_corner(right, left):
        return jnp.concatenate(
            [jnp.where(low_lanes, right, left), roll_lanes(jnp.where(low_lanes, left, right), 64)], axis=0)

    def fill_window(window, mine, columns, rows, corners):
        quarter = mine.shape[0] // 4
        side = unpack_columns(columns[0], columns[1])
        ends = unpack_rows(rows[0], rows[1])
        above = unpack_corner(corners[0], corners[1])
        below = unpack_corner(corners[2], corners[3])
        edge = unpack_rows(above, below)
        for m in range(4):
            part = slice(m * quarter, (m + 1) * quarter)
            window[0, part] = jnp.where(low_half, mine[part], ends[m])
            window[1, part] = jnp.where(low_half, side[m], edge[m])

    small[0].wait()
    for i in range(4):
        blocks[i].wait()
        for j in (0, 2):
            smooth(s_ref, i, j, x_ref, True)
    pl.semaphore_wait(barrier, across * along - 1)
    send_faces(0)

    coefficients = own[...]
    ssend[RIGHT] = pack_columns(coefficients, 1)
    ssend[LEFT] = pack_columns(coefficients, 0)
    ssend[UP] = pack_rows(coefficients, 1)
    ssend[DOWN] = pack_rows(coefficients, 0)
    for direction, source, keep_low in (
        (RIGHT_UP, UP, False), (RIGHT_DOWN, DOWN, False), (LEFT_UP, UP, True), (LEFT_DOWN, DOWN, True)
    ):
        dssend[direction - 4] = pack_corner(ssend[source], keep_low)
    for direction in range(8):
        send(*static_message(direction))
    for stage in range(3):
        for direction in range(4):
            clear(direction, frecv.at[stage, direction])
    for stage in range(2):
        for direction in range(4):
            clear(direction, erecv.at[stage, direction])
        for direction in range(4, 8):
            clear(direction, drecv.at[stage, direction - 4])
    for direction in range(4):
        clear(direction, srecv.at[direction])
    for direction in range(4, 8):
        clear(direction, dsrecv.at[direction - 4])

    residual()
    add_halo(0)
    smooth_all(x_ref)
    send_faces(1)
    residual()
    for direction in range(4):
        sent(*fine_message(0, direction))
    for direction in range(8):
        sent(*static_message(direction))
    for direction in range(8):
        arrived(*static_message(direction))
    fill_window(
        wst, own,
        (srecv[LEFT], srecv[RIGHT]), (srecv[DOWN], srecv[UP]),
        (dsrecv[LEFT_DOWN - 4], dsrecv[RIGHT_DOWN - 4], dsrecv[LEFT_UP - 4], dsrecv[RIGHT_UP - 4]),
    )
    add_halo(1)

    near_low, far_low = halves(1.0, NEAR), halves(FAR, 0.0)
    near_high, far_high = halves(NEAR, 1.0), halves(0.0, FAR)

    for a in range(5):
        for ip in range(2):
            if ip == 0:
                x = res[a, 0] + NEAR * res[a, 1] + FAR * res[a, 2]
            else:
                x = FAR * res[a, 1] + NEAR * res[a, 2] + res[a, 3]
            for jp in range(2):
                if jp == 0:
                    y = x[0] + NEAR * x[1] + FAR * x[2]
                else:
                    y = FAR * x[1] + NEAR * x[2] + x[3]
                z0 = near_low * y[0] + far_low * y[1]
                z1 = far_high * y[0] + near_high * y[1]
                n = a * 8 + ip * 4 + jp * 2
                fin[n] = z0 + roll_rows(z0, 4)
                fin[n + 1] = z1 + roll_rows(z1, 4)

    def exchange(stage, field, faces):
        nodes = faces.reshape(5, 2, 2, 2, 8, 128)
        x_low, x_up = nodes[:, 0].reshape(20, 8, 128), nodes[:, 1].reshape(20, 8, 128)
        y_low, y_up = nodes[:, :, 0].reshape(20, 8, 128), nodes[:, :, 1].reshape(20, 8, 128)
        esend[stage, RIGHT, 0:10] = pack_columns(field, 1)
        esend[stage, RIGHT, 10:15] = pack_columns(roll_lanes(x_up, EZ), 1)
        esend[stage, LEFT, 0:10] = pack_columns(field, 0)
        esend[stage, LEFT, 10:15] = pack_columns(roll_lanes(x_low, -EZ), 0)
        esend[stage, UP, 0:10] = pack_rows(field, 1)
        esend[stage, UP, 10:15] = pack_rows(roll_rows(y_up, 1), 1)
        esend[stage, DOWN, 0:10] = pack_rows(field, 0)
        esend[stage, DOWN, 10:15] = pack_rows(roll_rows(y_low, -1), 0)
        for direction, source, keep_low in (
            (RIGHT_UP, UP, False), (RIGHT_DOWN, DOWN, False), (LEFT_UP, UP, True), (LEFT_DOWN, DOWN, True)
        ):
            dsend[stage, direction - 4] = pack_corner(esend[stage, source, 0:10], keep_low)
        for direction in (4, 5, 6, 7, 0, 1, 2, 3):
            send(*coarse_message(stage, direction))

    def receive(stage, window, field):
        for direction in range(8):
            arrived(*coarse_message(stage, direction))
        fill_window(
            window, field,
            (erecv[stage, LEFT, 0:10], erecv[stage, RIGHT, 0:10]),
            (erecv[stage, DOWN, 0:10], erecv[stage, UP, 0:10]),
            (drecv[stage, LEFT_DOWN - 4], drecv[stage, RIGHT_DOWN - 4],
             drecv[stage, LEFT_UP - 4], drecv[stage, RIGHT_UP - 4]),
        )
        side = unpack_columns(erecv[stage, LEFT, 10:15], erecv[stage, RIGHT, 10:15])
        ends = unpack_rows(erecv[stage, DOWN, 10:15], erecv[stage, UP, 10:15])
        for m in range(4):
            wrx[5 * m:5 * m + 5] = side[m]
            wry[5 * m:5 * m + 5] = ends[m]

    strip_right = jnp.logical_and(low_half, lane // EZ == 1)
    strip_left = jnp.logical_and(low_half, lane // EZ == 2)

    def across_x(low0, low1, up0, up1, strip):
        l0, l1 = roll_lanes(low0, -EZ), roll_lanes(low1, -EZ)
        u0, u1 = roll_lanes(up0, EZ), roll_lanes(up1, EZ)
        not_last, first = lane < 128 - EZ, lane < EZ
        next0, next1 = jnp.where(not_last, l0, l1), jnp.where(not_last, l1, l0)
        prior0, prior1 = jnp.where(first, u1, u0), jnp.where(first, u0, u1)
        if strip is not None:
            next1 = jnp.where(strip_right, strip, next1)
            prior1 = jnp.where(strip_left, strip, prior1)
        return (next0, next1), (prior0, prior1)

    def window_faces(a, use_strips):
        tiles = [wm[tile, pl.ds(a * 8, 8)] for tile in range(2)]
        nodes = [u.reshape(2, 2, 2, 8, 128) for u in tiles]
        x_low, x_up = [u[0].reshape(4, 8, 128) for u in nodes], [u[1].reshape(4, 8, 128) for u in nodes]
        y_low, y_up = [u[:, 0].reshape(4, 8, 128) for u in nodes], [u[:, 1].reshape(4, 8, 128) for u in nodes]
        z_low, z_up = [u[:, :, 0].reshape(4, 8, 128) for u in nodes], [u[:, :, 1].reshape(4, 8, 128) for u in nodes]
        x_next, x_prior = across_x(
            x_low[0], x_low[1], x_up[0], x_up[1], wrx[pl.ds(a * 4, 4)] if use_strips else None)
        out = []
        for tile in range(2):
            px, py, pz = wst[tile, 101], wst[tile, 102], wst[tile, 103]
            x = (px * (x_low[tile] - x_prior[tile]), px * (x_up[tile] - x_next[tile]))
            y_next, y_prior = roll_rows(y_low[tile], -1), roll_rows(y_up[tile], 1)
            if tile == 0 and use_strips:
                strip = wry[pl.ds(a * 4, 4)]
                y_next = jnp.where(row == 5, strip, y_next)
                y_prior = jnp.where(row == 6, strip, y_prior)
            y = (py * (y_low[tile] - y_prior), py * (y_up[tile] - y_next))
            z = (pz * (z_low[tile] - has_prior * roll_lanes(z_up[tile], 1)),
                 pz * (z_up[tile] - has_next * roll_lanes(z_low[tile], -1)))
            slopes = (x_up[tile] - x_low[tile], y_up[tile] - y_low[tile], z_up[tile] - z_low[tile])
            out.append((tiles[tile], x, y, z, slopes))
        return out

    def fluxes(tiles):
        def one(n, c):
            d, tile = n // tiles, n % tiles
            slopes = [wsl[tile, d, b] for b in range(5)]
            totals = []
            for a in range(5):
                total = wst[tile, d * 25 + a * 5] * slopes[0]
                for b in range(1, 5):
                    total = total + wst[tile, d * 25 + a * 5 + b] * slopes[b]
                totals.append(total)
            for a in range(5):
                wc[tile, d, a] = totals[a]
            return c
        lax.fori_loop(0, 3 * tiles, one, 0)

    def middle_residual(use_strips):
        def one(a, c):
            rest = []
            for tile, (u, x, y, z, slopes) in enumerate(window_faces(a, use_strips)):
                r = ws[tile, pl.ds(a * 8, 8)] - wst[tile, 100] * u
                r = r.reshape(2, 2, 2, 8, 128)
                r = r - jnp.stack(x, axis=0).reshape(2, 2, 2, 8, 128)
                r = r - jnp.stack([v.reshape(2, 2, 8, 128) for v in y], axis=1)
                r = r - jnp.stack([v.reshape(2, 2, 8, 128) for v in z], axis=2)
                rest.append((r.reshape(8, 8, 128), slopes))
            for tile, (r, slopes) in enumerate(rest):
                wres[tile, a] = r
                for d in range(3):
                    wsl[tile, d, a] = slopes[d]
            return c
        lax.fori_loop(0, 5, one, 0)
        fluxes(2)

    def full_residual(tile, ip, a):
        r = wres[tile, a, pl.ds(ip * 4, 4)].reshape(2, 2, 8, 128)
        r = r - wc[tile, 0, a].reshape(2, 2, 8, 128)
        r = r - wc[tile, 1, a, pl.ds(ip * 2, 2)][None]
        return r - wc[tile, 2, a, pl.ds(ip * 2, 2)][:, None]

    def element_product(tile, values):
        out = []
        for a in range(5):
            total = wst[tile, 75 + a * 5] * values[0]
            for b in range(1, 5):
                total = total + wst[tile, 75 + a * 5 + b] * values[b]
            out.append(total)
        return out

    def middle_sweep(use_strips):
        middle_residual(use_strips)

        def one(n, c):
            tile, ip = n // 2, n % 2
            r = [full_residual(tile, ip, a).reshape(4, 8, 128) for a in range(5)]
            parts = [pl.ds(a * 8 + ip * 4, 4) for a in range(5)]
            totals = [wm[tile, part] + change for part, change in zip(parts, element_product(tile, r))]
            for part, total in zip(parts, totals):
                wm[tile, part] = total
            return c
        lax.fori_loop(0, 4, one, 0)

    def own_guess(n, c):
        part = [fin[pl.ds(b * 8 + n * 4, 4)] for b in range(5)]
        for a, value in enumerate(element_product(0, part)):
            fin[pl.ds(40 + a * 8 + n * 4, 4)] = value
        return c
    lax.fori_loop(0, 2, own_guess, 0)
    exchange(0, fin[0:40], fin[40:80])
    receive(0, ws, fin[0:40])

    def first_guess(n, c):
        tile, ip = n // 2, n % 2
        part = [ws[tile, pl.ds(b * 8 + ip * 4, 4)] for b in range(5)]
        for a, value in enumerate(element_product(tile, part)):
            wm[tile, pl.ds(a * 8 + ip * 4, 4)] = value
        return c
    lax.fori_loop(0, 4, first_guess, 0)
    middle_sweep(True)
    middle_residual(False)

    for tile in range(2):
        def bottom_source(a, c, tile=tile):
            total = full_residual(tile, 0, a) + full_residual(tile, 1, a)
            total = total[0] + total[1]
            wb[0, tile, a] = total[0] + total[1]
            return c
        lax.fori_loop(0, 5, bottom_source, 0)
    for tile in range(2):
        values = [wb[0, tile, a] for a in range(5)]
        for a, value in enumerate(element_product(tile, values)):
            wb[1, tile, a] = value
    bottom = wb[1, 0]
    (x_next, _), (x_prior, _) = across_x(bottom, wb[1, 1], bottom, wb[1, 1], None)
    applied = (time + 2.0 * (pen_x + pen_y + pen_z)) * bottom
    applied = applied - pen_x * (x_next + x_prior)
    applied = applied - pen_y * (roll_rows(bottom, 1) + roll_rows(bottom, -1))
    applied = applied - pen_z * (has_prior * roll_lanes(bottom, 1) + has_next * roll_lanes(bottom, -1))
    rest = wb[0, 0] - applied
    change = element_product(0, [rest[b] for b in range(5)])
    for a in range(5):
        fin[a * 8:a * 8 + 8] = wm[0, a * 8:a * 8 + 8] + (bottom[a] + change[a])

    exchange(1, fin[0:40], fin[0:40])
    receive(1, wm, fin[0:40])
    middle_sweep(True)
    middle_sweep(False)

    def final_parts(a, c):
        u, x, y, z, slopes = window_faces(a, False)[0]
        for d in range(3):
            wsl[0, d, a] = slopes[d]
        wres[0, a] = wst[0, 100] * u
        for d, terms in enumerate((x, y, z)):
            for side in range(2):
                fin[pl.ds((d * 2 + side) * 20 + a * 4, 4)] = terms[side]
        return c
    lax.fori_loop(0, 5, final_parts, 0)
    fluxes(1)

    def both(value):
        return jnp.where(low_half, value, roll_rows(value, 4))

    low_a, low_b = halves(1.0, NEAR), halves(0.0, FAR)
    high_a, high_b = halves(FAR, 0.0), halves(NEAR, 1.0)

    def spread_z(v0, v1):
        return low_a * v0 + low_b * v1, high_a * v0 + high_b * v1

    def spread_line(v0, v1):
        return v0, NEAR * v0 + FAR * v1, FAR * v0 + NEAR * v1, v1

    def prolong(value):
        value = both(value)
        z0, z1 = spread_z(value[:, :, 0], value[:, :, 1])
        pairs = jnp.stack([z0, z1], axis=2)
        lines = jnp.stack(spread_line(pairs[:, 0], pairs[:, 1]), axis=1)
        return spread_line(lines[0], lines[1])

    def final_fine(a, c):
        guess = [x_ref[a, i] + value
                 for i, value in enumerate(prolong(wm[0, pl.ds(a * 8, 8)].reshape(2, 2, 2, 8, 128)))]
        volume = wres[0, a].reshape(2, 2, 2, 8, 128) + wc[0, 0, a].reshape(1, 2, 2, 8, 128)
        volume = volume + wc[0, 1, a].reshape(2, 1, 2, 8, 128) + wc[0, 2, a].reshape(2, 2, 1, 8, 128)
        rest = [[[res[a, i, j, k2] - value[j, k2] for k2 in range(2)] for j in range(4)]
                for i, value in enumerate(prolong(volume))]
        for side in range(2):
            end = 3 * side
            face = both(fin[pl.ds(side * 20 + a * 4, 4)].reshape(2, 2, 8, 128))
            z = jnp.stack(spread_z(face[:, 0], face[:, 1]), axis=1)
            for m, value in enumerate(spread_line(z[0], z[1])):
                for k2 in range(2):
                    rest[end][m][k2] = rest[end][m][k2] - value[k2]
            face = both(fin[pl.ds((2 + side) * 20 + a * 4, 4)].reshape(2, 2, 8, 128))
            z = jnp.stack(spread_z(face[:, 0], face[:, 1]), axis=1)
            for m, value in enumerate(spread_line(z[0], z[1])):
                for k2 in range(2):
                    rest[m][end][k2] = rest[m][end][k2] - value[k2]
            face = fin[pl.ds((4 + side) * 20 + a * 4, 4)].reshape(2, 2, 8, 128)
            face = lower * face if side == 0 else upper * roll_rows(face, 4)
            lines = jnp.stack(spread_line(face[:, 0], face[:, 1]), axis=1)
            for m, value in enumerate(spread_line(lines[0], lines[1])):
                for n in range(4):
                    rest[m][n][side] = rest[m][n][side] - value[n]
        for i in range(4):
            x_ref[a, i] = guess[i]
            for j in range(4):
                for k2 in range(2):
                    res[a, i, j, k2] = rest[i][j][k2]
        return c
    lax.fori_loop(0, 5, final_fine, 0)
    smooth_all(x_ref)

    send_faces(2)
    residual()
    for stage in range(2):
        for direction in range(8):
            sent(*coarse_message(stage, direction))
    for direction in range(4):
        sent(*fine_message(1, direction))
    add_halo(2)
    smooth_all(out_ref)

    for direction in range(4):
        sent(*fine_message(2, direction))


def solution(mesh):
    sec_count, dom_count = mesh.shape["sec"], mesh.shape["dom"]

    def on_device(defect, point_inverse, flux_jacobian, time_term, penalty, element_inverse):
        def run(*refs):
            kernel(sec_count, dom_count, *refs)

        vmem = lambda *shape: pltpu.VMEM(shape + (8, 128), F32)
        dma = lambda *shape: pltpu.SemaphoreType.DMA(shape)
        out = pl.pallas_call(
            run,
            out_shape=jax.ShapeDtypeStruct((5, 4, 4, 2, 8, 128), F32),
            in_specs=[pl.BlockSpec(memory_space=pltpu.HBM)] * 6,
            out_specs=pl.BlockSpec(memory_space=pltpu.VMEM),
            scratch_shapes=[
                vmem(5, 4, 4, 2), vmem(5, 5, 4, 4, 2), pltpu.VMEM((75, 4, 128), F32), pltpu.VMEM((4, 128), F32),
                pltpu.VMEM((3, 4, 128), F32), pltpu.VMEM((25, 4, 128), F32),
                vmem(5, 4, 4, 2), vmem(100), vmem(104), vmem(2, 4, 2), vmem(5, 4, 4, 2),
                vmem(3, 4, 5, 2), vmem(3, 4, 5, 2), vmem(4, 26), vmem(4, 26),
                vmem(2, 4, 15), vmem(2, 4, 15), vmem(2, 4, 5), vmem(2, 4, 5), vmem(4, 13), vmem(4, 13),
                vmem(2, 104), vmem(2, 40), vmem(2, 40), vmem(2, 5, 8), vmem(2, 3, 5, 4), vmem(2, 3, 5, 4),
                vmem(20), vmem(20), vmem(2, 2, 5), vmem(120),
                dma(3, 4), dma(3, 4), dma(8), dma(8), dma(2, 8), dma(2, 8), dma(9),
            ],
            compiler_params=pltpu.CompilerParams(
                collective_id=0, has_side_effects=True, vmem_limit_bytes=48 << 20
            ),
        )(
            *(
                pltpu.with_memory_space_constraint(array, pltpu.HBM)
                for array in (
                    defect.reshape(5, 4, 4, 2, 8, 128),
                    point_inverse.reshape(5, 5, 4, 4, 2, 8, 128),
                    flux_jacobian.reshape(75, 4, 128),
                    time_term,
                    penalty,
                    element_inverse.reshape(25, 4, 128),
                )
            )
        )
        return out.reshape(5, 64, 4, 128)

    placed = (
        P(None, None, "sec", "dom"),
        P(None, None, None, "sec", "dom"),
        P(None, None, None, "sec", "dom"),
        P("sec", "dom"),
        P(None, "sec", "dom"),
        P(None, None, "sec", "dom"),
    )
    return jax.shard_map(
        on_device,
        mesh=mesh,
        in_specs=placed,
        out_specs=P(None, None, "sec", "dom"),
        check_vma=False,
    )
```

```python
import jax
import jax.numpy as jnp
import numpy as np
from jax import lax
from jax.experimental import pallas as pl
from jax.experimental.pallas import tpu as pltpu
from jax.sharding import PartitionSpec as P

EZ = 32
DAMPING = 0.7
MESH = pl.DeviceIdType.MESH
F32 = jnp.float32

STEPS = ((1, 0), (-1, 0), (0, 1), (0, -1), (1, 1), (1, -1), (-1, 1), (-1, -1))
RIGHT, LEFT, UP, DOWN, RIGHT_UP, RIGHT_DOWN, LEFT_UP, LEFT_DOWN = range(8)


def node_tables():
    points = np.array([-1.0, -1.0 / np.sqrt(5.0), 1.0 / np.sqrt(5.0), 1.0])
    barycentric = np.array(
        [1.0 / np.prod([points[j] - points[k] for k in range(4) if k != j]) for j in range(4)]
    )
    derivative = np.zeros((4, 4))
    for i in range(4):
        for j in range(4):
            if i != j:
                derivative[i, j] = barycentric[j] / barycentric[i] / (points[i] - points[j])
        derivative[i, i] = -np.sum(derivative[i])
    return derivative, (1.0 - points[1]) / 2.0, (1.0 + points[1]) / 2.0


DERIVATIVE, NEAR, FAR = node_tables()
EVEN = [float((DERIVATIVE[i, 0] + DERIVATIVE[i, 3]) / 2.0) for i in (0, 1)]
ODD = [[float((DERIVATIVE[i, j] - DERIVATIVE[i, 3 - j]) / 2.0) for j in (0, 1)] for i in (0, 1)]
NEAR, FAR = float(NEAR), float(FAR)


def roll_lanes(value, shift):
    shift %= 128
    return value if shift == 0 else pltpu.roll(value, shift, value.ndim - 1)


def roll_rows(value, shift):
    shift %= 8
    return value if shift == 0 else pltpu.roll(value, shift, value.ndim - 2)


def repeat(count, body):
    for n in range(count):
        body(n, 0)


def kernel(
    sec_count, dom_count,
    s_hbm, b_hbm, j_hbm, t_hbm, p_hbm, e_hbm,
    out_ref,
    s_ref, b_ref, j_ref, t_ref, p_ref, e_ref,
    x_ref, jd, own, dg, res,
    fsend, frecv, ssend, srecv, esend, erecv, dsend, drecv, dssend, dsrecv,
    wst, wm, ws, w48, wres, wc, wrx, wry, wb, fin,
    f_ss, f_rs, s_ss, s_rs, e_ss, e_rs, in_sem,
):
    small = [
        pltpu.make_async_copy(source, kept, in_sem.at[4 + n])
        for n, (source, kept) in enumerate(
            ((s_hbm, s_ref), (j_hbm, j_ref), (e_hbm, e_ref), (t_hbm, t_ref), (p_hbm, p_ref)))
    ]
    blocks = [
        pltpu.make_async_copy(b_hbm.at[:, :, i], b_ref.at[:, :, i], in_sem.at[i]) for i in range(4)
    ]
    for transfer in [small[0], blocks[0], blocks[3], blocks[1], blocks[2]] + small[1:]:
        transfer.start()
    me_sec, me_dom = lax.axis_index("sec"), lax.axis_index("dom")
    has_dom = {0: None, 1: me_dom < dom_count - 1, -1: me_dom > 0}
    has_sec = {0: None, 1: me_sec < sec_count - 1, -1: me_sec > 0}

    def exists(dx, dy):
        a, b = has_dom[dx], has_sec[dy]
        if a is None:
            return b
        if b is None:
            return a
        return jnp.logical_and(a, b)

    def target(direction):
        dx, dy = STEPS[direction]
        return (me_sec + dy, me_dom + dx)

    barrier = pltpu.get_barrier_semaphore()
    for direction in range(8):
        @pl.when(exists(*STEPS[direction]))
        def _(direction=direction):
            pl.semaphore_signal(barrier, inc=1, device_id=target(direction), device_id_type=MESH)
    one, zero = jnp.int32(1), jnp.int32(0)
    across = jnp.where(me_dom < dom_count - 1, one, zero) + jnp.where(me_dom > 0, one, zero) + 1
    along = jnp.where(me_sec < sec_count - 1, one, zero) + jnp.where(me_sec > 0, one, zero) + 1

    def copy(direction, src, dst, send_sem, recv_sem):
        return pltpu.make_async_remote_copy(
            src_ref=src, dst_ref=dst, send_sem=send_sem, recv_sem=recv_sem,
            device_id=target(direction), device_id_type=MESH,
        )

    def send(direction, src, dst, send_sem, recv_sem):
        @pl.when(exists(*STEPS[direction]))
        def _():
            copy(direction, src, dst, send_sem, recv_sem).start()

    def sent(direction, src, dst, send_sem, recv_sem):
        @pl.when(exists(*STEPS[direction]))
        def _():
            copy(direction, src, dst, send_sem, recv_sem).wait_send()

    def arrived(direction, src, dst, send_sem, recv_sem):
        dx, dy = STEPS[direction]

        @pl.when(exists(-dx, -dy))
        def _():
            copy(direction, src, dst, send_sem, recv_sem).wait_recv()

    def clear(direction, dst):
        dx, dy = STEPS[direction]

        @pl.when(jnp.logical_not(exists(-dx, -dy)))
        def _():
            dst[...] = jnp.zeros_like(dst)

    def fine_message(stage, direction):
        return (direction, fsend.at[stage, direction], frecv.at[stage, direction],
                f_ss.at[stage, direction], f_rs.at[stage, direction])

    def static_message(direction):
        if direction < 4:
            src, dst = ssend.at[direction], srecv.at[direction]
        else:
            src, dst = dssend.at[direction - 4], dsrecv.at[direction - 4]
        return direction, src, dst, s_ss.at[direction], s_rs.at[direction]

    def coarse_message(stage, direction):
        if direction < 4:
            part = pl.ds(0, (15, 14)[stage])
            src, dst = esend.at[stage, direction, part], erecv.at[stage, direction, part]
        else:
            part = pl.ds(0, (5, 6)[stage])
            src, dst = dsend.at[stage, direction - 4, part], drecv.at[stage, direction - 4, part]
        return direction, src, dst, e_ss.at[stage, direction], e_rs.at[stage, direction]

    lane = lax.broadcasted_iota(jnp.int32, (8, 128), 1)
    row = lax.broadcasted_iota(jnp.int32, (8, 128), 0)
    low_half = row < 4
    low_lanes = lane < 64
    z_index = lane % EZ
    has_next = jnp.where(z_index < EZ - 1, 1.0, 0.0)
    has_prior = jnp.where(z_index > 0, 1.0, 0.0)
    lower = jnp.where(low_half, 1.0, 0.0)
    upper = 1.0 - lower
    row4 = row % 4

    def halves(a, b):
        return jnp.where(low_half, F32(a), F32(b))

    def smooth(source, i, j, target, first):
        part = pl.ds(j, 2)
        values = [source[a, i, part] for a in range(5)]
        totals = []
        for a in range(5):
            total = b_ref[a, 0, i, part] * values[0]
            for b in range(1, 5):
                total = total + b_ref[a, b, i, part] * values[b]
            total = DAMPING * total
            totals.append(total if first else x_ref[a, i, part] + total)
        for a in range(5):
            target[a, i, part] = totals[a]

    def smooth_slab(source, i, target, first=False):
        for j in (0, 2):
            smooth(source, i, j, target, first)

    def pieces(face, rolled, place):
        packed = None
        for m in range(4):
            piece = rolled(face(m), m)
            packed = piece if packed is None else jnp.where(place == m, piece, packed)
        return packed

    def send_x_faces(stage):
        fsend[stage, RIGHT] = pieces(
            lambda m: x_ref[:, 3, m], lambda v, m: roll_lanes(v, EZ * (m + 1)), lane // EZ)
        fsend[stage, LEFT] = pieces(
            lambda m: x_ref[:, 0, m], lambda v, m: roll_lanes(v, EZ * m), lane // EZ)
        for direction in (RIGHT, LEFT):
            send(*fine_message(stage, direction))

    def send_y_faces(stage):
        fsend[stage, UP] = pieces(
            lambda m: x_ref[:, m, 3], lambda v, m: roll_rows(v, m - 3), row4)
        fsend[stage, DOWN] = pieces(
            lambda m: x_ref[:, m, 0], lambda v, m: roll_rows(v, m), row4)
        for direction in (UP, DOWN):
            send(*fine_message(stage, direction))

    even_z = halves(EVEN[0], EVEN[1])
    even_z_swapped = halves(EVEN[1], EVEN[0])
    odd_z = halves(ODD[0][0], ODD[1][1])
    odd_z_cross = halves(ODD[0][1], ODD[1][0])
    odd_z_swapped = halves(ODD[1][1], ODD[0][0])
    odd_z_cross_swapped = halves(ODD[1][0], ODD[0][1])

    def jacobian(d, parts):
        out = []
        for a in range(5):
            total = [jd[d * 25 + a * 5] * value for value in parts[0]]
            for b in range(1, 5):
                block = jd[d * 25 + a * 5 + b]
                total = [t + block * value for t, value in zip(total, parts[b])]
            out.append(total)
        return out

    def line_parts(u):
        return [u[0] - u[3], u[1] - u[2], (u[0] + u[3]) - (u[1] + u[2])]

    def line_slopes(outer, inner, even):
        e0, e1 = EVEN[0] * even, EVEN[1] * even
        o0 = ODD[0][0] * outer + ODD[0][1] * inner
        o1 = ODD[1][0] * outer + ODD[1][1] * inner
        return o0 + e0, o1 + e1, o1 - e1, o0 - e0

    def residual():
        def along_x(n, c):
            j, k2 = n // 2, n % 2
            inner_weight, outer_weight = dg[0, j, k2], dg[1, j, k2]
            u = [x_ref[a, :, j, k2] for a in range(5)]
            flux = jacobian(0, [line_parts(v) for v in u])
            out = []
            for a in range(5):
                slopes = line_slopes(*flux[a])
                s = s_ref[a, :, j, k2]
                v = u[a]
                out.append(jnp.stack([
                    (s[0] - outer_weight * v[0]) + (px_prior * roll_lanes(v[3], EZ) - slopes[0]),
                    (s[1] - inner_weight * v[1]) - slopes[1],
                    (s[2] - inner_weight * v[2]) - slopes[2],
                    (s[3] - outer_weight * v[3]) + (px_next * roll_lanes(v[0], -EZ) - slopes[3]),
                ]))
            for a in range(5):
                res[a, :, j, k2] = out[a]
            return c
        repeat(8, along_x)

        def along_y(n, c):
            i, k2 = n // 2, n % 2
            u = [x_ref[a, i, :, k2] for a in range(5)]
            flux = jacobian(1, [line_parts(v) for v in u])
            out = []
            for a in range(5):
                slopes = line_slopes(*flux[a])
                r = res[a, i, :, k2]
                v = u[a]
                out.append(jnp.stack([
                    r[0] + (py_prior * roll_rows(v[3], 1) - slopes[0]),
                    r[1] - slopes[1],
                    r[2] - slopes[2],
                    r[3] + (py_next * roll_rows(v[0], -1) - slopes[3]),
                ]))
            for a in range(5):
                res[a, i, :, k2] = out[a]
            return c
        repeat(8, along_y)

        def along_z(n, c):
            i, j = n // 2, 2 * (n % 2)
            part = pl.ds(j, 2)
            parts, adds = [], []
            for a in range(5):
                u = x_ref[a, i, part]
                v0, v1 = u[:, 0], u[:, 1]
                w0, w1 = roll_rows(v0, 4), roll_rows(v1, 4)
                straight, swapped = v0 + w1, w0 + v1
                odd = v0 - w1
                even = jnp.where(low_half, straight[0] - swapped[0], swapped[1] - straight[1])
                parts.append([odd[0], odd[1], even])
                adds.append(jnp.stack([pz_prior * roll_lanes(w1, 1), pz_next * roll_lanes(w0, -1)], axis=1))
            flux = jacobian(2, parts)
            out = []
            for a in range(5):
                turned = roll_rows(flux[a][2], 4)
                even = (jnp.where(low_half, flux[a][2], turned), jnp.where(low_half, turned, flux[a][2]))
                lines = []
                for m in range(2):
                    odd = flux[a][m]
                    cross = roll_rows(odd, 4)
                    lines.append(jnp.stack([
                        odd_z * odd + odd_z_cross * cross + even_z * even[m],
                        odd_z_swapped * cross + odd_z_cross_swapped * odd - even_z_swapped * even[m],
                    ]))
                out.append(res[a, i, part] + (adds[a] - jnp.stack(lines)))
            for a in range(5):
                res[a, i, part] = out[a]
            return c
        repeat(8, along_z)

    def add_y_halo(stage):
        for direction in (UP, DOWN):
            arrived(*fine_message(stage, direction))
        from_below, from_above = frecv[stage, UP], frecv[stage, DOWN]
        for m in range(4):
            res[:, m, 0] = res[:, m, 0] + py_below * roll_rows(from_below, -m)
            res[:, m, 3] = res[:, m, 3] + py_above * roll_rows(from_above, 3 - m)

    def add_x_halo(stage):
        for direction in (RIGHT, LEFT):
            arrived(*fine_message(stage, direction))
        from_left, from_right = frecv[stage, RIGHT], frecv[stage, LEFT]
        for m in range(4):
            res[:, 0, m] = res[:, 0, m] + px_left * roll_lanes(from_left, -EZ * m)
            res[:, 3, m] = res[:, 3, m] + px_right * roll_lanes(from_right, 128 - EZ * (m + 1))

    def finish_sweep(stage, target):
        add_y_halo(stage)
        for i in (1, 2):
            smooth_slab(res, i, target)
        add_x_halo(stage)
        for i in (0, 3):
            smooth_slab(res, i, target)

    def pack_columns(value, first_block):
        quarter = value.shape[0] // 4
        packed = None
        for m in range(4):
            piece = roll_rows(roll_lanes(value[m * quarter:(m + 1) * quarter], 64 * (m % 2)), 4 * (m // 2))
            place = jnp.logical_and(row // 4 == m // 2, lane // 64 == (first_block + m) % 2)
            packed = piece if packed is None else jnp.where(place, piece, packed)
        return packed

    def pack_rows(value, first_pair):
        quarter = value.shape[0] // 4
        packed = None
        for m in range(4):
            piece = roll_rows(value[m * quarter:(m + 1) * quarter], 2 * m)
            packed = piece if packed is None else jnp.where(row // 2 == (first_pair + m) % 4, piece, packed)
        return packed

    def pack_corner(rows_packed, keep_low):
        half = rows_packed.shape[0] // 2
        return jnp.where(low_lanes == keep_low, rows_packed[:half], roll_lanes(rows_packed[half:], 64))

    def unpack_columns(from_right, from_left):
        out = []
        for m in range(4):
            both = jnp.where(lane // 64 == m % 2, from_right, from_left)
            out.append(roll_rows(roll_lanes(both, -64 * (m % 2)), -4 * (m // 2)))
        return out

    def unpack_rows(from_above, from_below):
        return [roll_rows(jnp.where(row // 2 == m, from_above, from_below), 4 - 2 * m) for m in range(4)]

    def unpack_corner(right, left):
        return jnp.concatenate(
            [jnp.where(low_lanes, right, left), roll_lanes(jnp.where(low_lanes, left, right), 64)], axis=0)

    def fill_near(window, mine, rows):
        quarter = mine.shape[0] // 4
        ends = unpack_rows(rows[0], rows[1])
        for m in range(4):
            part = slice(m * quarter, (m + 1) * quarter)
            window[0, part] = jnp.where(low_half, mine[part], ends[m])

    def fill_far(window, columns, corners):
        quarter = columns[0].shape[0]
        side = unpack_columns(columns[0], columns[1])
        above = unpack_corner(corners[0], corners[1])
        below = unpack_corner(corners[2], corners[3])
        edge = unpack_rows(above, below)
        for m in range(4):
            window[1, m * quarter:(m + 1) * quarter] = jnp.where(low_half, side[m], edge[m])

    small[0].wait()
    for i in (0, 3):
        blocks[i].wait()
        smooth_slab(s_ref, i, x_ref, True)
    pl.semaphore_wait(barrier, across * along - 1)
    send_x_faces(0)
    for i in (1, 2):
        blocks[i].wait()
        smooth_slab(s_ref, i, x_ref, True)
    send_y_faces(0)

    for transfer in small[1:]:
        transfer.wait()
    for array, start, count, scale in ((j_ref, 0, 75, 0.5), (e_ref, 75, 25, DAMPING)):
        value = array[...]
        jd[start:start + count, 0:4] = value
        jd[start:start + count, 4:8] = value
    own[0:75] = 0.5 * jd[0:75]
    own[75:100] = DAMPING * jd[75:100]
    for n, value in enumerate((t_ref[...], p_ref[0], p_ref[1], p_ref[2])):
        own[100 + n, 0:4] = value
        own[100 + n, 4:8] = value
    time, pen_x, pen_y, pen_z = own[100], own[101], own[102], own[103]
    for f in range(2):
        for j in range(4):
            for k2 in range(2):
                total = time + pen_z * (lower if k2 == 0 else upper)
                if j in (0, 3):
                    total = total + pen_y
                dg[f, j, k2] = total + pen_x if f else total

    px_prior = jnp.where(lane >= EZ, pen_x, 0.0)
    px_next = jnp.where(lane < 128 - EZ, pen_x, 0.0)
    px_left = jnp.where(lane < EZ, pen_x, 0.0)
    px_right = jnp.where(lane >= 128 - EZ, pen_x, 0.0)
    py_prior = jnp.where(row4 != 0, pen_y, 0.0)
    py_next = jnp.where(row4 != 3, pen_y, 0.0)
    py_below = jnp.where(row4 == 0, pen_y, 0.0)
    py_above = jnp.where(row4 == 3, pen_y, 0.0)
    pz_prior = pen_z * lower * has_prior
    pz_next = pen_z * upper * has_next

    coefficients = own[...]
    ssend[RIGHT] = pack_columns(coefficients, 1)
    ssend[LEFT] = pack_columns(coefficients, 0)
    ssend[UP] = pack_rows(coefficients, 1)
    ssend[DOWN] = pack_rows(coefficients, 0)
    for direction, source, keep_low in (
        (RIGHT_UP, UP, False), (RIGHT_DOWN, DOWN, False), (LEFT_UP, UP, True), (LEFT_DOWN, DOWN, True)
    ):
        dssend[direction - 4] = pack_corner(ssend[source], keep_low)
    for direction in range(8):
        send(*static_message(direction))
    for stage in range(3):
        for direction in range(4):
            clear(direction, frecv.at[stage, direction])
    for stage in range(2):
        for direction in range(4):
            clear(direction, erecv.at[stage, direction])
        for direction in range(4, 8):
            clear(direction, drecv.at[stage, direction - 4])
    for direction in range(4):
        clear(direction, srecv.at[direction])
    for direction in range(4, 8):
        clear(direction, dsrecv.at[direction - 4])

    residual()
    finish_sweep(0, x_ref)
    send_x_faces(1)
    send_y_faces(1)
    residual()
    for direction in range(4):
        sent(*fine_message(0, direction))
    for direction in range(8):
        sent(*static_message(direction))
    for direction in range(8):
        arrived(*static_message(direction))
    fill_near(wst, own, (srecv[DOWN], srecv[UP]))
    fill_far(
        wst, (srecv[LEFT], srecv[RIGHT]),
        (dsrecv[LEFT_DOWN - 4], dsrecv[RIGHT_DOWN - 4], dsrecv[LEFT_UP - 4], dsrecv[RIGHT_UP - 4]),
    )
    add_y_halo(1)
    add_x_halo(1)

    near_low, far_low = halves(1.0, NEAR), halves(FAR, 0.0)
    near_high, far_high = halves(NEAR, 1.0), halves(0.0, FAR)

    for a in range(5):
        for ip in range(2):
            if ip == 0:
                x = res[a, 0] + NEAR * res[a, 1] + FAR * res[a, 2]
            else:
                x = FAR * res[a, 1] + NEAR * res[a, 2] + res[a, 3]
            for jp in range(2):
                if jp == 0:
                    y = x[0] + NEAR * x[1] + FAR * x[2]
                else:
                    y = FAR * x[1] + NEAR * x[2] + x[3]
                z0 = near_low * y[0] + far_low * y[1]
                z1 = far_high * y[0] + near_high * y[1]
                n = a * 8 + ip * 4 + jp * 2
                fin[n] = z0 + roll_rows(z0, 4)
                fin[n + 1] = z1 + roll_rows(z1, 4)

    CORNERS = ((RIGHT_UP, UP, False), (RIGHT_DOWN, DOWN, False), (LEFT_UP, UP, True), (LEFT_DOWN, DOWN, True))

    def exchange(stage, field, x_prior, x_next, y_prior, y_next):
        main = field.shape[0] // 4
        whole = main + x_prior.shape[0] // 4
        esend[stage, UP, 0:main] = pack_rows(field, 1)
        esend[stage, DOWN, 0:main] = pack_rows(field, 0)
        for direction, source, keep_low in CORNERS:
            dsend[stage, direction - 4, 0:main // 2] = pack_corner(esend[stage, source, 0:main], keep_low)
        for direction, _, _ in CORNERS:
            send(*coarse_message(stage, direction))
        esend[stage, RIGHT, 0:main] = pack_columns(field, 1)
        esend[stage, RIGHT, main:whole] = pack_columns(x_prior, 1)
        esend[stage, LEFT, 0:main] = pack_columns(field, 0)
        esend[stage, LEFT, main:whole] = pack_columns(x_next, 0)
        for direction in (RIGHT, LEFT):
            send(*coarse_message(stage, direction))
        esend[stage, UP, main:whole] = pack_rows(y_prior, 1)
        esend[stage, DOWN, main:whole] = pack_rows(y_next, 0)
        for direction in (UP, DOWN):
            send(*coarse_message(stage, direction))

    def receive_near(stage, window, field, strips):
        main, more = field.shape[0] // 4, strips // 4
        for direction in (UP, DOWN):
            arrived(*coarse_message(stage, direction))
        fill_near(window, field, (erecv[stage, DOWN, 0:main], erecv[stage, UP, 0:main]))
        ends = unpack_rows(erecv[stage, DOWN, main:main + more], erecv[stage, UP, main:main + more])
        for m in range(4):
            wry[more * m:more * m + more] = ends[m]

    def receive_far(stage, window, fields, strips):
        main, more = fields // 4, strips // 4
        for direction in (RIGHT, LEFT, RIGHT_UP, RIGHT_DOWN, LEFT_UP, LEFT_DOWN):
            arrived(*coarse_message(stage, direction))
        half = main // 2
        fill_far(
            window, (erecv[stage, LEFT, 0:main], erecv[stage, RIGHT, 0:main]),
            (drecv[stage, LEFT_DOWN - 4, 0:half], drecv[stage, RIGHT_DOWN - 4, 0:half],
             drecv[stage, LEFT_UP - 4, 0:half], drecv[stage, RIGHT_UP - 4, 0:half]),
        )
        side = unpack_columns(erecv[stage, LEFT, main:main + more], erecv[stage, RIGHT, main:main + more])
        for m in range(4):
            wrx[more * m:more * m + more] = side[m]

    strip_right = jnp.logical_and(low_half, lane // EZ == 1)
    strip_left = jnp.logical_and(low_half, lane // EZ == 2)

    def across_x(low0, low1, up0, up1, strip):
        l0, l1 = roll_lanes(low0, -EZ), roll_lanes(low1, -EZ)
        u0, u1 = roll_lanes(up0, EZ), roll_lanes(up1, EZ)
        not_last, first = lane < 128 - EZ, lane < EZ
        next0, next1 = jnp.where(not_last, l0, l1), jnp.where(not_last, l1, l0)
        prior0, prior1 = jnp.where(first, u1, u0), jnp.where(first, u0, u1)
        if strip is not None:
            next1 = jnp.where(strip_right, strip, next1)
            prior1 = jnp.where(strip_left, strip, prior1)
        return (next0, next1), (prior0, prior1)

    def window_faces(a, use_strips):
        tiles = [wm[tile, pl.ds(a * 8, 8)] for tile in range(2)]
        nodes = [u.reshape(2, 2, 2, 8, 128) for u in tiles]
        x_low, x_up = [u[0].reshape(4, 8, 128) for u in nodes], [u[1].reshape(4, 8, 128) for u in nodes]
        y_low, y_up = [u[:, 0].reshape(4, 8, 128) for u in nodes], [u[:, 1].reshape(4, 8, 128) for u in nodes]
        z_low, z_up = [u[:, :, 0].reshape(4, 8, 128) for u in nodes], [u[:, :, 1].reshape(4, 8, 128) for u in nodes]
        x_next, x_prior = across_x(
            x_low[0], x_low[1], x_up[0], x_up[1], wrx[pl.ds(a * 4, 4)] if use_strips else None)
        out = []
        for tile in range(2):
            px, py, pz = wst[tile, 101], wst[tile, 102], wst[tile, 103]
            x = (px * (x_low[tile] - x_prior[tile]), px * (x_up[tile] - x_next[tile]))
            y_next, y_prior = roll_rows(y_low[tile], -1), roll_rows(y_up[tile], 1)
            if tile == 0 and use_strips:
                strip = wry[pl.ds(a * 4, 4)]
                y_next = jnp.where(row == 5, strip, y_next)
                y_prior = jnp.where(row == 6, strip, y_prior)
            y = (py * (y_low[tile] - y_prior), py * (y_up[tile] - y_next))
            z = (pz * (z_low[tile] - has_prior * roll_lanes(z_up[tile], 1)),
                 pz * (z_up[tile] - has_next * roll_lanes(z_low[tile], -1)))
            out.append((tiles[tile], x, y, z))
        return out

    def fluxes(tile):
        slopes = ([], [], [])
        for a in range(5):
            u = wm[tile, a * 8:a * 8 + 8].reshape(2, 2, 2, 8, 128)
            slopes[0].append((u[1] - u[0]).reshape(4, 8, 128))
            slopes[1].append((u[:, 1] - u[:, 0]).reshape(4, 8, 128))
            slopes[2].append((u[:, :, 1] - u[:, :, 0]).reshape(4, 8, 128))
        for d in range(3):
            for a in range(5):
                total = wst[tile, d * 25 + a * 5] * slopes[d][0]
                for b in range(1, 5):
                    total = total + wst[tile, d * 25 + a * 5 + b] * slopes[d][b]
                wc[tile, d, a] = total

    def middle_faces(use_strips):
        for a in range(5):
            for tile, (u, x, y, z) in enumerate(window_faces(a, use_strips)):
                r = ws[tile, a * 8:a * 8 + 8] - wst[tile, 100] * u
                r = r.reshape(2, 2, 2, 8, 128)
                r = r - jnp.stack(x, axis=0).reshape(2, 2, 2, 8, 128)
                r = r - jnp.stack([v.reshape(2, 2, 8, 128) for v in y], axis=1)
                r = r - jnp.stack([v.reshape(2, 2, 8, 128) for v in z], axis=2)
                wres[tile, a] = r.reshape(8, 8, 128)

    def full_residual(tile, ip, a):
        r = wres[tile, a, pl.ds(ip * 4, 4)].reshape(2, 2, 8, 128)
        r = r - wc[tile, 0, a].reshape(2, 2, 8, 128)
        r = r - wc[tile, 1, a, pl.ds(ip * 2, 2)][None]
        return r - wc[tile, 2, a, pl.ds(ip * 2, 2)][:, None]

    def element_product(tile, values):
        out = []
        for a in range(5):
            total = wst[tile, 75 + a * 5] * values[0]
            for b in range(1, 5):
                total = total + wst[tile, 75 + a * 5 + b] * values[b]
            out.append(total)
        return out

    def middle_update():
        for tile in range(2):
            for ip in range(2):
                r = [full_residual(tile, ip, a).reshape(4, 8, 128) for a in range(5)]
                parts = [pl.ds(a * 8 + ip * 4, 4) for a in range(5)]
                for part, change in zip(parts, element_product(tile, r)):
                    wm[tile, part] = wm[tile, part] + change

    def first_guess(tile):
        for ip in range(2):
            part = [ws[tile, pl.ds(b * 8 + ip * 4, 4)] for b in range(5)]
            for a, value in enumerate(element_product(tile, part)):
                wm[tile, pl.ds(a * 8 + ip * 4, 4)] = value

    for ip in range(2):
        part = [fin[pl.ds(b * 8 + ip * 4, 4)] for b in range(5)]
        for a, value in enumerate(element_product(0, part)):
            fin[pl.ds(40 + a * 8 + ip * 4, 4)] = value
    nodes = fin[40:80].reshape(5, 2, 2, 2, 8, 128)
    exchange(
        0, fin[0:40],
        roll_lanes(nodes[:, 1].reshape(20, 8, 128), EZ), roll_lanes(nodes[:, 0].reshape(20, 8, 128), -EZ),
        roll_rows(nodes[:, :, 1].reshape(20, 8, 128), 1), roll_rows(nodes[:, :, 0].reshape(20, 8, 128), -1),
    )
    receive_near(0, ws, fin[0:40], 20)
    first_guess(0)
    fluxes(0)
    receive_far(0, ws, 40, 20)
    first_guess(1)
    fluxes(1)
    middle_faces(True)
    middle_update()
    for tile in range(2):
        fluxes(tile)
    middle_faces(False)

    for tile in range(2):
        source = []
        for a in range(5):
            parts = [full_residual(tile, ip, a) for ip in range(2)]
            if tile == 0:
                for ip in range(2):
                    fin[a * 8 + ip * 4:a * 8 + ip * 4 + 4] = parts[ip].reshape(4, 8, 128)
            total = parts[0] + parts[1]
            total = total[0] + total[1]
            source.append(total[0] + total[1])
            wb[0, tile, a] = source[a]
        for a, value in enumerate(element_product(tile, source)):
            wb[1, tile, a] = value
    bottom = wb[1, 0]
    (x_next, _), (x_prior, _) = across_x(bottom, wb[1, 1], bottom, wb[1, 1], None)
    applied = (time + 2.0 * (pen_x + pen_y + pen_z)) * bottom
    applied = applied - pen_x * (x_next + x_prior)
    applied = applied - pen_y * (roll_rows(bottom, 1) + roll_rows(bottom, -1))
    applied = applied - pen_z * (has_prior * roll_lanes(bottom, 1) + has_next * roll_lanes(bottom, -1))
    rest = wb[0, 0] - applied
    change = element_product(0, [rest[b] for b in range(5)])
    for a in range(5):
        fin[40 + a] = bottom[a] + change[a]
    for n in range(45, 48):
        fin[n] = jnp.zeros((8, 128), F32)

    guess = fin[40:48]
    exchange(
        1, fin[0:48], roll_lanes(guess, EZ), roll_lanes(guess, -EZ), roll_rows(guess, 1), roll_rows(guess, -1))

    def constant_terms(tile, b, y_next, y_prior):
        py, pz = wst[tile, 102], wst[tile, 103]
        y = (py * (b - y_prior), py * (b - y_next))
        z = (pz * (b - has_prior * roll_lanes(b, 1)), pz * (b - has_next * roll_lanes(b, -1)))
        base = wst[tile, 100] * b
        return [[(base + y[jp]) + z[kp] for kp in range(2)] for jp in range(2)]

    def add_bottom(tile, b, terms, x_terms):
        for ip in range(2):
            r = []
            for a in range(5):
                own_terms = jnp.stack([terms[jp][kp][a] for jp in range(2) for kp in range(2)])
                value = w48[tile, a * 8 + ip * 4:a * 8 + ip * 4 + 4] - own_terms
                r.append(value if x_terms is None else value - x_terms[ip][a])
            for a, change in enumerate(element_product(tile, r)):
                part = pl.ds(a * 8 + ip * 4, 4)
                wm[tile, part] = wm[tile, part] + (b[a] + change)

    receive_near(1, w48, fin[0:48], 8)
    b0 = w48[0, 40:45]
    y_next = jnp.where(row == 5, wry[0:5], roll_rows(b0, -1))
    y_prior = jnp.where(row == 6, wry[0:5], roll_rows(b0, 1))
    add_bottom(0, b0, constant_terms(0, b0, y_next, y_prior), None)
    receive_far(1, w48, 48, 8)
    b1 = w48[1, 40:45]
    x_next, x_prior = across_x(b0, b1, b0, b1, wrx[0:5])
    x_terms = [
        (wst[tile, 101] * (b - x_prior[tile]), wst[tile, 101] * (b - x_next[tile]))
        for tile, b in enumerate((b0, b1))
    ]
    for ip in range(2):
        change = element_product(0, [x_terms[0][ip][a] for a in range(5)])
        for a in range(5):
            part = pl.ds(a * 8 + ip * 4, 4)
            wm[0, part] = wm[0, part] - change[a]
    add_bottom(1, b1, constant_terms(1, b1, roll_rows(b1, -1), roll_rows(b1, 1)), x_terms[1])
    for tile in range(2):
        fluxes(tile)
    middle_faces(False)
    middle_update()

    def final_parts(a, c):
        u, x, y, z = window_faces(a, False)[0]
        wres[0, a] = wst[0, 100] * u
        for d, terms in enumerate((x, y, z)):
            for side in range(2):
                fin[(d * 2 + side) * 20 + a * 4:(d * 2 + side) * 20 + a * 4 + 4] = terms[side]
    for a in range(5):
        final_parts(a, 0)
    fluxes(0)

    def both(value):
        return jnp.where(low_half, value, roll_rows(value, 4))

    low_a, low_b = halves(1.0, NEAR), halves(0.0, FAR)
    high_a, high_b = halves(FAR, 0.0), halves(NEAR, 1.0)

    def spread_z(v0, v1):
        return low_a * v0 + low_b * v1, high_a * v0 + high_b * v1

    def spread_line(v0, v1):
        return v0, NEAR * v0 + FAR * v1, FAR * v0 + NEAR * v1, v1

    def prolong_lines(value):
        value = both(value)
        z0, z1 = spread_z(value[:, :, 0], value[:, :, 1])
        pairs = jnp.stack([z0, z1], axis=2)
        return jnp.stack(spread_line(pairs[:, 0], pairs[:, 1]), axis=1)

    def between(lines, i):
        if i in (0, 3):
            return lines[i // 3]
        near, far = (0, 1) if i == 1 else (1, 0)
        return NEAR * lines[near] + FAR * lines[far]

    def face_lines(a, d, side):
        face = both(fin[(d * 2 + side) * 20 + a * 4:(d * 2 + side) * 20 + a * 4 + 4].reshape(2, 2, 8, 128))
        return jnp.stack(spread_z(face[:, 0], face[:, 1]), axis=1)

    def final_slabs(slabs):
        for a in range(5):
            guess, volume = lines_of[a]
            y_faces, z_faces = faces_of[a]
            for i in slabs:
                x_ref[a, i] = x_ref[a, i] + between(guess, i)
                value = res[a, i] - between(volume, i)
                if i in (0, 3):
                    z = face_lines(a, 0, i // 3)
                    value = value - jnp.stack(spread_line(z[0], z[1]))
                y = [between(face, i) for face in y_faces]
                z = jnp.stack([between(face, i) for face in z_faces], axis=1)
                value = value - z
                res[a, i] = jnp.concatenate([(value[0] - y[0])[None], value[1:3], (value[3] - y[1])[None]])

    lines_of, faces_of = [], []
    for a in range(5):
        volume = wres[0, a].reshape(2, 2, 2, 8, 128) + wc[0, 0, a].reshape(1, 2, 2, 8, 128)
        volume = volume + wc[0, 1, a].reshape(2, 1, 2, 8, 128) + wc[0, 2, a].reshape(2, 2, 1, 8, 128)
        lines_of.append((prolong_lines(wm[0, a * 8:a * 8 + 8].reshape(2, 2, 2, 8, 128)), prolong_lines(volume)))
        y_faces = [face_lines(a, 1, side) for side in range(2)]
        z_faces = []
        for side in range(2):
            face = fin[(4 + side) * 20 + a * 4:(4 + side) * 20 + a * 4 + 4].reshape(2, 2, 8, 128)
            face = lower * face if side == 0 else upper * roll_rows(face, 4)
            z_faces.append(jnp.stack(spread_line(face[:, 0], face[:, 1]), axis=1))
        faces_of.append((y_faces, z_faces))
    final_slabs((0, 3))
    for i in (0, 3):
        smooth_slab(res, i, x_ref)
    send_x_faces(2)
    final_slabs((1, 2))
    for i in (1, 2):
        smooth_slab(res, i, x_ref)
    send_y_faces(2)
    residual()
    for stage in range(2):
        for direction in range(8):
            sent(*coarse_message(stage, direction))
    for direction in range(4):
        sent(*fine_message(1, direction))
    finish_sweep(2, out_ref)
    for direction in range(4):
        sent(*fine_message(2, direction))


def solution(mesh):
    sec_count, dom_count = mesh.shape["sec"], mesh.shape["dom"]

    def on_device(defect, point_inverse, flux_jacobian, time_term, penalty, element_inverse):
        def run(*refs):
            kernel(sec_count, dom_count, *refs)

        vmem = lambda *shape: pltpu.VMEM(shape + (8, 128), F32)
        dma = lambda *shape: pltpu.SemaphoreType.DMA(shape)
        out = pl.pallas_call(
            run,
            out_shape=jax.ShapeDtypeStruct((5, 4, 4, 2, 8, 128), F32),
            in_specs=[pl.BlockSpec(memory_space=pltpu.HBM)] * 6,
            out_specs=pl.BlockSpec(memory_space=pltpu.VMEM),
            scratch_shapes=[
                vmem(5, 4, 4, 2), vmem(5, 5, 4, 4, 2), pltpu.VMEM((75, 4, 128), F32), pltpu.VMEM((4, 128), F32),
                pltpu.VMEM((3, 4, 128), F32), pltpu.VMEM((25, 4, 128), F32),
                vmem(5, 4, 4, 2), vmem(100), vmem(104), vmem(2, 4, 2), vmem(5, 4, 4, 2),
                vmem(3, 4, 5, 2), vmem(3, 4, 5, 2), vmem(4, 26), vmem(4, 26),
                vmem(2, 4, 15), vmem(2, 4, 15), vmem(2, 4, 6), vmem(2, 4, 6), vmem(4, 13), vmem(4, 13),
                vmem(2, 104), vmem(2, 40), vmem(2, 40), vmem(2, 48), vmem(2, 5, 8), vmem(2, 3, 5, 4),
                vmem(20), vmem(20), vmem(2, 2, 5), vmem(120),
                dma(3, 4), dma(3, 4), dma(8), dma(8), dma(2, 8), dma(2, 8), dma(9),
            ],
            compiler_params=pltpu.CompilerParams(
                collective_id=0, has_side_effects=True, vmem_limit_bytes=48 << 20
            ),
        )(
            *(
                pltpu.with_memory_space_constraint(array, pltpu.HBM)
                for array in (
                    defect.reshape(5, 4, 4, 2, 8, 128),
                    point_inverse.reshape(5, 5, 4, 4, 2, 8, 128),
                    flux_jacobian.reshape(75, 4, 128),
                    time_term,
                    penalty,
                    element_inverse.reshape(25, 4, 128),
                )
            )
        )
        return out.reshape(5, 64, 4, 128)

    placed = (
        P(None, None, "sec", "dom"),
        P(None, None, None, "sec", "dom"),
        P(None, None, None, "sec", "dom"),
        P("sec", "dom"),
        P(None, "sec", "dom"),
        P(None, None, "sec", "dom"),
    )
    return jax.shard_map(
        on_device,
        mesh=mesh,
        in_specs=placed,
        out_specs=P(None, None, "sec", "dom"),
        check_vma=False,
    )
```

```python
import jax
import jax.numpy as jnp
import numpy as np
from jax import lax
from jax.experimental import pallas as pl
from jax.experimental.pallas import tpu as pltpu
from jax.sharding import PartitionSpec as P

EZ = 32
DAMPING = 0.7
MESH = pl.DeviceIdType.MESH
F32 = jnp.float32

STEPS = ((1, 0), (-1, 0), (0, 1), (0, -1), (1, 1), (1, -1), (-1, 1), (-1, -1))
RIGHT, LEFT, UP, DOWN, RIGHT_UP, RIGHT_DOWN, LEFT_UP, LEFT_DOWN = range(8)


def node_tables():
    points = np.array([-1.0, -1.0 / np.sqrt(5.0), 1.0 / np.sqrt(5.0), 1.0])
    barycentric = np.array(
        [1.0 / np.prod([points[j] - points[k] for k in range(4) if k != j]) for j in range(4)]
    )
    derivative = np.zeros((4, 4))
    for i in range(4):
        for j in range(4):
            if i != j:
                derivative[i, j] = barycentric[j] / barycentric[i] / (points[i] - points[j])
        derivative[i, i] = -np.sum(derivative[i])
    return derivative, (1.0 - points[1]) / 2.0, (1.0 + points[1]) / 2.0


DERIVATIVE, NEAR, FAR = node_tables()
EVEN = [float((DERIVATIVE[i, 0] + DERIVATIVE[i, 3]) / 2.0) for i in (0, 1)]
ODD = [[float((DERIVATIVE[i, j] - DERIVATIVE[i, 3 - j]) / 2.0) for j in (0, 1)] for i in (0, 1)]
NEAR, FAR = float(NEAR), float(FAR)


def roll_lanes(value, shift):
    shift %= 128
    return value if shift == 0 else pltpu.roll(value, shift, value.ndim - 1)


def roll_rows(value, shift):
    shift %= 8
    return value if shift == 0 else pltpu.roll(value, shift, value.ndim - 2)


def repeat(count, body):
    for n in range(count):
        body(n, 0)


def kernel(
    sec_count, dom_count,
    s_hbm, b_hbm, j_hbm, t_hbm, p_hbm, e_hbm,
    out_ref,
    s_ref, b_ref, j_ref, t_ref, p_ref, e_ref,
    x_ref, jd, own, dg, res,
    fsend, frecv, ssend, srecv, esend, erecv, dsend, drecv, dssend, dsrecv,
    wst, wdg, wm, ws, w48, wres, wc, wrx, wry, wb, fin,
    f_ss, f_rs, s_ss, s_rs, e_ss, e_rs, in_sem,
):
    small = [
        pltpu.make_async_copy(source, kept, in_sem.at[4 + n])
        for n, (source, kept) in enumerate(
            ((s_hbm, s_ref), (j_hbm, j_ref), (e_hbm, e_ref), (t_hbm, t_ref), (p_hbm, p_ref)))
    ]
    blocks = [
        pltpu.make_async_copy(b_hbm.at[:, :, i], b_ref.at[:, :, i], in_sem.at[i]) for i in range(4)
    ]
    for transfer in [small[0], blocks[0], blocks[3], blocks[1], blocks[2]] + small[1:]:
        transfer.start()
    me_sec, me_dom = lax.axis_index("sec"), lax.axis_index("dom")
    has_dom = {0: None, 1: me_dom < dom_count - 1, -1: me_dom > 0}
    has_sec = {0: None, 1: me_sec < sec_count - 1, -1: me_sec > 0}

    def exists(dx, dy):
        a, b = has_dom[dx], has_sec[dy]
        if a is None:
            return b
        if b is None:
            return a
        return jnp.logical_and(a, b)

    def target(direction):
        dx, dy = STEPS[direction]
        return (me_sec + dy, me_dom + dx)

    barrier = pltpu.get_barrier_semaphore()
    for direction in range(8):
        @pl.when(exists(*STEPS[direction]))
        def _(direction=direction):
            pl.semaphore_signal(barrier, inc=1, device_id=target(direction), device_id_type=MESH)
    one, zero = jnp.int32(1), jnp.int32(0)
    across = jnp.where(me_dom < dom_count - 1, one, zero) + jnp.where(me_dom > 0, one, zero) + 1
    along = jnp.where(me_sec < sec_count - 1, one, zero) + jnp.where(me_sec > 0, one, zero) + 1

    def copy(direction, src, dst, send_sem, recv_sem):
        return pltpu.make_async_remote_copy(
            src_ref=src, dst_ref=dst, send_sem=send_sem, recv_sem=recv_sem,
            device_id=target(direction), device_id_type=MESH,
        )

    def send(direction, src, dst, send_sem, recv_sem):
        @pl.when(exists(*STEPS[direction]))
        def _():
            copy(direction, src, dst, send_sem, recv_sem).start()

    def sent(direction, src, dst, send_sem, recv_sem):
        @pl.when(exists(*STEPS[direction]))
        def _():
            copy(direction, src, dst, send_sem, recv_sem).wait_send()

    def arrived(direction, src, dst, send_sem, recv_sem):
        dx, dy = STEPS[direction]

        @pl.when(exists(-dx, -dy))
        def _():
            copy(direction, src, dst, send_sem, recv_sem).wait_recv()

    def clear(direction, dst):
        dx, dy = STEPS[direction]

        @pl.when(jnp.logical_not(exists(-dx, -dy)))
        def _():
            dst[...] = jnp.zeros_like(dst)

    def fine_message(stage, direction):
        return (direction, fsend.at[stage, direction], frecv.at[stage, direction],
                f_ss.at[stage, direction], f_rs.at[stage, direction])

    def static_message(direction):
        if direction < 4:
            src, dst = ssend.at[direction], srecv.at[direction]
        else:
            src, dst = dssend.at[direction - 4], dsrecv.at[direction - 4]
        return direction, src, dst, s_ss.at[direction], s_rs.at[direction]

    def coarse_message(stage, direction):
        if direction < 4:
            part = pl.ds(0, (15, 14)[stage])
            src, dst = esend.at[stage, direction, part], erecv.at[stage, direction, part]
        else:
            part = pl.ds(0, (5, 6)[stage])
            src, dst = dsend.at[stage, direction - 4, part], drecv.at[stage, direction - 4, part]
        return direction, src, dst, e_ss.at[stage, direction], e_rs.at[stage, direction]

    lane = lax.broadcasted_iota(jnp.int32, (8, 128), 1)
    row = lax.broadcasted_iota(jnp.int32, (8, 128), 0)
    low_half = row < 4
    low_lanes = lane < 64
    z_index = lane % EZ
    has_next = jnp.where(z_index < EZ - 1, 1.0, 0.0)
    has_prior = jnp.where(z_index > 0, 1.0, 0.0)
    lower = jnp.where(low_half, 1.0, 0.0)
    upper = 1.0 - lower
    row4 = row % 4

    def halves(a, b):
        return jnp.where(low_half, F32(a), F32(b))

    def smooth(source, i, j, target, first):
        part = pl.ds(j, 2)
        values = [source[a, i, part] for a in range(5)]
        totals = []
        for a in range(5):
            total = b_ref[a, 0, i, part] * values[0]
            for b in range(1, 5):
                total = total + b_ref[a, b, i, part] * values[b]
            total = DAMPING * total
            totals.append(total if first else x_ref[a, i, part] + total)
        for a in range(5):
            target[a, i, part] = totals[a]

    def smooth_slab(source, i, target, first=False):
        for j in (0, 2):
            smooth(source, i, j, target, first)

    def pieces(face, rolled, place):
        packed = None
        for m in range(4):
            piece = rolled(face(m), m)
            packed = piece if packed is None else jnp.where(place == m, piece, packed)
        return packed

    def send_x_faces(stage):
        fsend[stage, RIGHT] = pieces(
            lambda m: x_ref[:, 3, m], lambda v, m: roll_lanes(v, EZ * (m + 1)), lane // EZ)
        fsend[stage, LEFT] = pieces(
            lambda m: x_ref[:, 0, m], lambda v, m: roll_lanes(v, EZ * m), lane // EZ)
        for direction in (RIGHT, LEFT):
            send(*fine_message(stage, direction))

    def send_y_faces(stage):
        fsend[stage, UP] = pieces(
            lambda m: x_ref[:, m, 3], lambda v, m: roll_rows(v, m - 3), row4)
        fsend[stage, DOWN] = pieces(
            lambda m: x_ref[:, m, 0], lambda v, m: roll_rows(v, m), row4)
        for direction in (UP, DOWN):
            send(*fine_message(stage, direction))

    even_z = halves(EVEN[0], EVEN[1])
    even_z_swapped = halves(EVEN[1], EVEN[0])
    odd_z = halves(ODD[0][0], ODD[1][1])
    odd_z_cross = halves(ODD[0][1], ODD[1][0])
    odd_z_swapped = halves(ODD[1][1], ODD[0][0])
    odd_z_cross_swapped = halves(ODD[1][0], ODD[0][1])

    def jacobian(d, parts):
        out = []
        for a in range(5):
            total = [jd[d * 25 + a * 5] * value for value in parts[0]]
            for b in range(1, 5):
                block = jd[d * 25 + a * 5 + b]
                total = [t + block * value for t, value in zip(total, parts[b])]
            out.append(total)
        return out

    def line_parts(u):
        return [u[0] - u[3], u[1] - u[2], (u[0] + u[3]) - (u[1] + u[2])]

    def line_slopes(outer, inner, even):
        e0, e1 = EVEN[0] * even, EVEN[1] * even
        o0 = ODD[0][0] * outer + ODD[0][1] * inner
        o1 = ODD[1][0] * outer + ODD[1][1] * inner
        return o0 + e0, o1 + e1, o1 - e1, o0 - e0

    def residual():
        def along_x(n, c):
            j, k2 = n // 2, n % 2
            inner_weight, outer_weight = dg[0, j, k2], dg[1, j, k2]
            u = [x_ref[a, :, j, k2] for a in range(5)]
            flux = jacobian(0, [line_parts(v) for v in u])
            out = []
            for a in range(5):
                slopes = line_slopes(*flux[a])
                s = s_ref[a, :, j, k2]
                v = u[a]
                out.append(jnp.stack([
                    (s[0] - outer_weight * v[0]) + (px_prior * roll_lanes(v[3], EZ) - slopes[0]),
                    (s[1] - inner_weight * v[1]) - slopes[1],
                    (s[2] - inner_weight * v[2]) - slopes[2],
                    (s[3] - outer_weight * v[3]) + (px_next * roll_lanes(v[0], -EZ) - slopes[3]),
                ]))
            for a in range(5):
                res[a, :, j, k2] = out[a]
            return c
        repeat(8, along_x)

        def along_y(n, c):
            i, k2 = n // 2, n % 2
            u = [x_ref[a, i, :, k2] for a in range(5)]
            flux = jacobian(1, [line_parts(v) for v in u])
            out = []
            for a in range(5):
                slopes = line_slopes(*flux[a])
                r = res[a, i, :, k2]
                v = u[a]
                out.append(jnp.stack([
                    r[0] + (py_prior * roll_rows(v[3], 1) - slopes[0]),
                    r[1] - slopes[1],
                    r[2] - slopes[2],
                    r[3] + (py_next * roll_rows(v[0], -1) - slopes[3]),
                ]))
            for a in range(5):
                res[a, i, :, k2] = out[a]
            return c
        repeat(8, along_y)

        def along_z(n, c):
            i, j = n // 2, 2 * (n % 2)
            part = pl.ds(j, 2)
            parts, adds = [], []
            for a in range(5):
                u = x_ref[a, i, part]
                v0, v1 = u[:, 0], u[:, 1]
                w0, w1 = roll_rows(v0, 4), roll_rows(v1, 4)
                straight, swapped = v0 + w1, w0 + v1
                odd = v0 - w1
                even = jnp.where(low_half, straight[0] - swapped[0], swapped[1] - straight[1])
                parts.append([odd[0], odd[1], even])
                adds.append(jnp.stack([pz_prior * roll_lanes(w1, 1), pz_next * roll_lanes(w0, -1)], axis=1))
            flux = jacobian(2, parts)
            out = []
            for a in range(5):
                turned = roll_rows(flux[a][2], 4)
                even = (jnp.where(low_half, flux[a][2], turned), jnp.where(low_half, turned, flux[a][2]))
                lines = []
                for m in range(2):
                    odd = flux[a][m]
                    cross = roll_rows(odd, 4)
                    lines.append(jnp.stack([
                        odd_z * odd + odd_z_cross * cross + even_z * even[m],
                        odd_z_swapped * cross + odd_z_cross_swapped * odd - even_z_swapped * even[m],
                    ]))
                out.append(res[a, i, part] + (adds[a] - jnp.stack(lines)))
            for a in range(5):
                res[a, i, part] = out[a]
            return c
        repeat(8, along_z)

    def add_y_halo(stage):
        for direction in (UP, DOWN):
            arrived(*fine_message(stage, direction))
        from_below, from_above = frecv[stage, UP], frecv[stage, DOWN]
        for m in range(4):
            res[:, m, 0] = res[:, m, 0] + py_below * roll_rows(from_below, -m)
            res[:, m, 3] = res[:, m, 3] + py_above * roll_rows(from_above, 3 - m)

    def add_x_halo(stage):
        for direction in (RIGHT, LEFT):
            arrived(*fine_message(stage, direction))
        from_left, from_right = frecv[stage, RIGHT], frecv[stage, LEFT]
        for m in range(4):
            res[:, 0, m] = res[:, 0, m] + px_left * roll_lanes(from_left, -EZ * m)
            res[:, 3, m] = res[:, 3, m] + px_right * roll_lanes(from_right, 128 - EZ * (m + 1))

    def finish_sweep(stage, target):
        add_y_halo(stage)
        for i in (1, 2):
            smooth_slab(res, i, target)
        add_x_halo(stage)
        for i in (0, 3):
            smooth_slab(res, i, target)

    def pack_columns(value, first_block):
        quarter = value.shape[0] // 4
        packed = None
        for m in range(4):
            piece = roll_rows(roll_lanes(value[m * quarter:(m + 1) * quarter], 64 * (m % 2)), 4 * (m // 2))
            place = jnp.logical_and(row // 4 == m // 2, lane // 64 == (first_block + m) % 2)
            packed = piece if packed is None else jnp.where(place, piece, packed)
        return packed

    def pack_rows(value, first_pair):
        quarter = value.shape[0] // 4
        packed = None
        for m in range(4):
            piece = roll_rows(value[m * quarter:(m + 1) * quarter], 2 * m)
            packed = piece if packed is None else jnp.where(row // 2 == (first_pair + m) % 4, piece, packed)
        return packed

    def pack_corner(rows_packed, keep_low):
        half = rows_packed.shape[0] // 2
        return jnp.where(low_lanes == keep_low, rows_packed[:half], roll_lanes(rows_packed[half:], 64))

    def unpack_columns(from_right, from_left):
        out = []
        for m in range(4):
            both = jnp.where(lane // 64 == m % 2, from_right, from_left)
            out.append(roll_rows(roll_lanes(both, -64 * (m % 2)), -4 * (m // 2)))
        return out

    def unpack_rows(from_above, from_below):
        return [roll_rows(jnp.where(row // 2 == m, from_above, from_below), 4 - 2 * m) for m in range(4)]

    def unpack_corner(right, left):
        return jnp.concatenate(
            [jnp.where(low_lanes, right, left), roll_lanes(jnp.where(low_lanes, left, right), 64)], axis=0)

    def fill_near(window, mine, rows):
        quarter = mine.shape[0] // 4
        ends = unpack_rows(rows[0], rows[1])
        for m in range(4):
            part = slice(m * quarter, (m + 1) * quarter)
            window[0, part] = jnp.where(low_half, mine[part], ends[m])

    def fill_far(window, columns, corners):
        quarter = columns[0].shape[0]
        side = unpack_columns(columns[0], columns[1])
        above = unpack_corner(corners[0], corners[1])
        below = unpack_corner(corners[2], corners[3])
        edge = unpack_rows(above, below)
        for m in range(4):
            window[1, m * quarter:(m + 1) * quarter] = jnp.where(low_half, side[m], edge[m])

    small[0].wait()
    for i in (0, 3):
        blocks[i].wait()
        smooth_slab(s_ref, i, x_ref, True)
    pl.semaphore_wait(barrier, across * along - 1)
    send_x_faces(0)
    for i in (1, 2):
        blocks[i].wait()
        smooth_slab(s_ref, i, x_ref, True)
    send_y_faces(0)

    for transfer in small[1:]:
        transfer.wait()
    for array, start, count, scale in ((j_ref, 0, 75, 0.5), (e_ref, 75, 25, DAMPING)):
        value = array[...]
        jd[start:start + count, 0:4] = value
        jd[start:start + count, 4:8] = value
    own[0:75] = 0.5 * jd[0:75]
    own[75:100] = DAMPING * jd[75:100]
    for n, value in enumerate((t_ref[...], p_ref[0], p_ref[1], p_ref[2])):
        own[100 + n, 0:4] = value
        own[100 + n, 4:8] = value
    time, pen_x, pen_y, pen_z = own[100], own[101], own[102], own[103]
    for f in range(2):
        for j in range(4):
            for k2 in range(2):
                total = time + pen_z * (lower if k2 == 0 else upper)
                if j in (0, 3):
                    total = total + pen_y
                dg[f, j, k2] = total + pen_x if f else total

    px_prior = jnp.where(lane >= EZ, pen_x, 0.0)
    px_next = jnp.where(lane < 128 - EZ, pen_x, 0.0)
    px_left = jnp.where(lane < EZ, pen_x, 0.0)
    px_right = jnp.where(lane >= 128 - EZ, pen_x, 0.0)
    py_prior = jnp.where(row4 != 0, pen_y, 0.0)
    py_next = jnp.where(row4 != 3, pen_y, 0.0)
    py_below = jnp.where(row4 == 0, pen_y, 0.0)
    py_above = jnp.where(row4 == 3, pen_y, 0.0)
    pz_prior = pen_z * lower * has_prior
    pz_next = pen_z * upper * has_next

    coefficients = own[...]
    ssend[RIGHT] = pack_columns(coefficients, 1)
    ssend[LEFT] = pack_columns(coefficients, 0)
    ssend[UP] = pack_rows(coefficients, 1)
    ssend[DOWN] = pack_rows(coefficients, 0)
    for direction, source, keep_low in (
        (RIGHT_UP, UP, False), (RIGHT_DOWN, DOWN, False), (LEFT_UP, UP, True), (LEFT_DOWN, DOWN, True)
    ):
        dssend[direction - 4] = pack_corner(ssend[source], keep_low)
    for direction in range(8):
        send(*static_message(direction))
    for stage in range(3):
        for direction in range(4):
            clear(direction, frecv.at[stage, direction])
    for stage in range(2):
        for direction in range(4):
            clear(direction, erecv.at[stage, direction])
        for direction in range(4, 8):
            clear(direction, drecv.at[stage, direction - 4])
    for direction in range(4):
        clear(direction, srecv.at[direction])
    for direction in range(4, 8):
        clear(direction, dsrecv.at[direction - 4])

    residual()
    finish_sweep(0, x_ref)
    send_x_faces(1)
    send_y_faces(1)
    residual()
    for direction in range(4):
        sent(*fine_message(0, direction))
    for direction in range(8):
        sent(*static_message(direction))
    for direction in range(8):
        arrived(*static_message(direction))
    fill_near(wst, own, (srecv[DOWN], srecv[UP]))
    fill_far(
        wst, (srecv[LEFT], srecv[RIGHT]),
        (dsrecv[LEFT_DOWN - 4], dsrecv[RIGHT_DOWN - 4], dsrecv[LEFT_UP - 4], dsrecv[RIGHT_UP - 4]),
    )
    for tile in range(2):
        px, py, pz = wst[tile, 101], wst[tile, 102], wst[tile, 103]
        wdg[tile, 0] = wst[tile, 100] + (px + py + pz)
        wdg[tile, 1] = pz * has_prior
        wdg[tile, 2] = pz * has_next
    add_y_halo(1)
    add_x_halo(1)

    near_low, far_low = halves(1.0, NEAR), halves(FAR, 0.0)
    near_high, far_high = halves(NEAR, 1.0), halves(0.0, FAR)

    for a in range(5):
        for ip in range(2):
            if ip == 0:
                x = res[a, 0] + NEAR * res[a, 1] + FAR * res[a, 2]
            else:
                x = FAR * res[a, 1] + NEAR * res[a, 2] + res[a, 3]
            for jp in range(2):
                if jp == 0:
                    y = x[0] + NEAR * x[1] + FAR * x[2]
                else:
                    y = FAR * x[1] + NEAR * x[2] + x[3]
                z0 = near_low * y[0] + far_low * y[1]
                z1 = far_high * y[0] + near_high * y[1]
                n = a * 8 + ip * 4 + jp * 2
                fin[n] = z0 + roll_rows(z0, 4)
                fin[n + 1] = z1 + roll_rows(z1, 4)

    CORNERS = ((RIGHT_UP, UP, False), (RIGHT_DOWN, DOWN, False), (LEFT_UP, UP, True), (LEFT_DOWN, DOWN, True))

    def exchange(stage, field, x_prior, x_next, y_prior, y_next):
        main = field.shape[0] // 4
        whole = main + x_prior.shape[0] // 4
        esend[stage, UP, 0:main] = pack_rows(field, 1)
        esend[stage, DOWN, 0:main] = pack_rows(field, 0)
        for direction, source, keep_low in CORNERS:
            dsend[stage, direction - 4, 0:main // 2] = pack_corner(esend[stage, source, 0:main], keep_low)
        for direction, _, _ in CORNERS:
            send(*coarse_message(stage, direction))
        esend[stage, RIGHT, 0:main] = pack_columns(field, 1)
        esend[stage, RIGHT, main:whole] = pack_columns(x_prior, 1)
        esend[stage, LEFT, 0:main] = pack_columns(field, 0)
        esend[stage, LEFT, main:whole] = pack_columns(x_next, 0)
        for direction in (RIGHT, LEFT):
            send(*coarse_message(stage, direction))
        esend[stage, UP, main:whole] = pack_rows(y_prior, 1)
        esend[stage, DOWN, main:whole] = pack_rows(y_next, 0)
        for direction in (UP, DOWN):
            send(*coarse_message(stage, direction))

    def receive_near(stage, window, field, strips):
        main, more = field.shape[0] // 4, strips // 4
        for direction in (UP, DOWN):
            arrived(*coarse_message(stage, direction))
        fill_near(window, field, (erecv[stage, DOWN, 0:main], erecv[stage, UP, 0:main]))
        ends = unpack_rows(erecv[stage, DOWN, main:main + more], erecv[stage, UP, main:main + more])
        for m in range(4):
            wry[more * m:more * m + more] = ends[m]

    def receive_far(stage, window, fields, strips):
        main, more = fields // 4, strips // 4
        for direction in (RIGHT, LEFT, RIGHT_UP, RIGHT_DOWN, LEFT_UP, LEFT_DOWN):
            arrived(*coarse_message(stage, direction))
        half = main // 2
        fill_far(
            window, (erecv[stage, LEFT, 0:main], erecv[stage, RIGHT, 0:main]),
            (drecv[stage, LEFT_DOWN - 4, 0:half], drecv[stage, RIGHT_DOWN - 4, 0:half],
             drecv[stage, LEFT_UP - 4, 0:half], drecv[stage, RIGHT_UP - 4, 0:half]),
        )
        side = unpack_columns(erecv[stage, LEFT, main:main + more], erecv[stage, RIGHT, main:main + more])
        for m in range(4):
            wrx[more * m:more * m + more] = side[m]

    strip_right = jnp.logical_and(low_half, lane // EZ == 1)
    strip_left = jnp.logical_and(low_half, lane // EZ == 2)

    def across_x(low0, low1, up0, up1, strip):
        l0, l1 = roll_lanes(low0, -EZ), roll_lanes(low1, -EZ)
        u0, u1 = roll_lanes(up0, EZ), roll_lanes(up1, EZ)
        not_last, first = lane < 128 - EZ, lane < EZ
        next0, next1 = jnp.where(not_last, l0, l1), jnp.where(not_last, l1, l0)
        prior0, prior1 = jnp.where(first, u1, u0), jnp.where(first, u0, u1)
        if strip is not None:
            next1 = jnp.where(strip_right, strip, next1)
            prior1 = jnp.where(strip_left, strip, prior1)
        return (next0, next1), (prior0, prior1)

    def neighbours(a, use_strips):
        tiles = [wm[tile, a * 8:a * 8 + 8] for tile in range(2)]
        nodes = [u.reshape(2, 2, 2, 8, 128) for u in tiles]
        x_low, x_up = [u[0].reshape(4, 8, 128) for u in nodes], [u[1].reshape(4, 8, 128) for u in nodes]
        y_low, y_up = [u[:, 0].reshape(4, 8, 128) for u in nodes], [u[:, 1].reshape(4, 8, 128) for u in nodes]
        z_low, z_up = [u[:, :, 0].reshape(4, 8, 128) for u in nodes], [u[:, :, 1].reshape(4, 8, 128) for u in nodes]
        x_next, x_prior = across_x(
            x_low[0], x_low[1], x_up[0], x_up[1], wrx[a * 4:a * 4 + 4] if use_strips else None)
        out = []
        for tile in range(2):
            y_next, y_prior = roll_rows(y_low[tile], -1), roll_rows(y_up[tile], 1)
            if tile == 0 and use_strips:
                strip = wry[a * 4:a * 4 + 4]
                y_next = jnp.where(row == 5, strip, y_next)
                y_prior = jnp.where(row == 6, strip, y_prior)
            out.append((
                tiles[tile], (x_prior[tile], x_next[tile]), (y_prior, y_next),
                (roll_lanes(z_up[tile], 1), roll_lanes(z_low[tile], -1)),
                ((x_low[tile], x_up[tile]), (y_low[tile], y_up[tile]), (z_low[tile], z_up[tile])),
            ))
        return out

    def fluxes(tile):
        slopes = ([], [], [])
        for a in range(5):
            u = wm[tile, a * 8:a * 8 + 8].reshape(2, 2, 2, 8, 128)
            slopes[0].append((u[1] - u[0]).reshape(4, 8, 128))
            slopes[1].append((u[:, 1] - u[:, 0]).reshape(4, 8, 128))
            slopes[2].append((u[:, :, 1] - u[:, :, 0]).reshape(4, 8, 128))
        for d in range(3):
            for a in range(5):
                total = wst[tile, d * 25 + a * 5] * slopes[d][0]
                for b in range(1, 5):
                    total = total + wst[tile, d * 25 + a * 5 + b] * slopes[d][b]
                wc[tile, d, a] = total

    def middle_faces(use_strips, tiles=2):
        for a in range(5):
            for tile, (u, x, y, z, _) in enumerate(neighbours(a, use_strips)[:tiles]):
                px, py = wst[tile, 101], wst[tile, 102]
                pz = (wdg[tile, 1], wdg[tile, 2])
                r = (ws[tile, a * 8:a * 8 + 8] - wdg[tile, 0] * u).reshape(2, 2, 2, 8, 128)
                r = r + jnp.stack([px * v for v in x], axis=0).reshape(2, 2, 2, 8, 128)
                r = r + jnp.stack([(py * v).reshape(2, 2, 8, 128) for v in y], axis=1)
                r = r + jnp.stack([(p * v).reshape(2, 2, 8, 128) for p, v in zip(pz, z)], axis=2)
                wres[tile, a] = r.reshape(8, 8, 128)

    def full_residual(tile, ip, a):
        r = wres[tile, a, pl.ds(ip * 4, 4)].reshape(2, 2, 8, 128)
        r = r - wc[tile, 0, a].reshape(2, 2, 8, 128)
        r = r - wc[tile, 1, a, pl.ds(ip * 2, 2)][None]
        return r - wc[tile, 2, a, pl.ds(ip * 2, 2)][:, None]

    def element_product(tile, values):
        out = []
        for a in range(5):
            total = wst[tile, 75 + a * 5] * values[0]
            for b in range(1, 5):
                total = total + wst[tile, 75 + a * 5 + b] * values[b]
            out.append(total)
        return out

    def middle_update():
        for tile in range(2):
            for ip in range(2):
                r = [full_residual(tile, ip, a).reshape(4, 8, 128) for a in range(5)]
                parts = [pl.ds(a * 8 + ip * 4, 4) for a in range(5)]
                for part, change in zip(parts, element_product(tile, r)):
                    wm[tile, part] = wm[tile, part] + change

    def first_guess(tile):
        for ip in range(2):
            part = [ws[tile, pl.ds(b * 8 + ip * 4, 4)] for b in range(5)]
            for a, value in enumerate(element_product(tile, part)):
                wm[tile, pl.ds(a * 8 + ip * 4, 4)] = value

    for ip in range(2):
        part = [fin[pl.ds(b * 8 + ip * 4, 4)] for b in range(5)]
        for a, value in enumerate(element_product(0, part)):
            fin[pl.ds(40 + a * 8 + ip * 4, 4)] = value
    nodes = fin[40:80].reshape(5, 2, 2, 2, 8, 128)
    exchange(
        0, fin[0:40],
        roll_lanes(nodes[:, 1].reshape(20, 8, 128), EZ), roll_lanes(nodes[:, 0].reshape(20, 8, 128), -EZ),
        roll_rows(nodes[:, :, 1].reshape(20, 8, 128), 1), roll_rows(nodes[:, :, 0].reshape(20, 8, 128), -1),
    )
    receive_near(0, ws, fin[0:40], 20)
    first_guess(0)
    fluxes(0)
    receive_far(0, ws, 40, 20)
    first_guess(1)
    fluxes(1)
    middle_faces(True)
    middle_update()
    fluxes(0)
    middle_faces(False, 1)

    def far_sources():
        rest, slopes = [], ([], [], [])
        for a in range(5):
            u = wm[1, a * 8:a * 8 + 8].reshape(2, 2, 2, 8, 128)
            v = wm[0, a * 8:a * 8 + 8].reshape(2, 4, 8, 128)
            pairs = u[:, :, 0] + u[:, :, 1]
            x_low, x_up = pairs[0, 0] + pairs[0, 1], pairs[1, 0] + pairs[1, 1]
            y_low, y_up = pairs[0, 0] + pairs[1, 0], pairs[0, 1] + pairs[1, 1]
            z = u[0] + u[1]
            z_low, z_up = z[0, 0] + z[1, 0], z[0, 1] + z[1, 1]
            near_low = (v[0, 0] + v[0, 1]) + (v[0, 2] + v[0, 3])
            near_up = (v[1, 0] + v[1, 1]) + (v[1, 2] + v[1, 3])
            (_, x_next), (_, x_prior) = across_x(near_low, x_low, near_up, x_up, None)
            total = ws[1, a * 8]
            for n in range(1, 8):
                total = total + ws[1, a * 8 + n]
            total = total - wdg[1, 0] * (x_low + x_up)
            total = total + wst[1, 101] * (x_next + x_prior)
            total = total + wst[1, 102] * (roll_rows(y_low, -1) + roll_rows(y_up, 1))
            total = total + (wdg[1, 1] * roll_lanes(z_up, 1) + wdg[1, 2] * roll_lanes(z_low, -1))
            rest.append(total)
            for d, slope in enumerate((x_up - x_low, y_up - y_low, z_up - z_low)):
                slopes[d].append(2.0 * slope)
        for a in range(5):
            for d in range(3):
                for b in range(5):
                    rest[a] = rest[a] - wst[1, d * 25 + a * 5 + b] * slopes[d][b]
        return rest

    def near_sources():
        source = []
        for a in range(5):
            parts = [full_residual(0, ip, a) for ip in range(2)]
            for ip in range(2):
                fin[a * 8 + ip * 4:a * 8 + ip * 4 + 4] = parts[ip].reshape(4, 8, 128)
            total = parts[0] + parts[1]
            total = total[0] + total[1]
            source.append(total[0] + total[1])
        return source

    for tile, source in enumerate((near_sources(), far_sources())):
        for a in range(5):
            wb[0, tile, a] = source[a]
        for a, value in enumerate(element_product(tile, source)):
            wb[1, tile, a] = value
    bottom = wb[1, 0]
    (x_next, _), (x_prior, _) = across_x(bottom, wb[1, 1], bottom, wb[1, 1], None)
    applied = (time + 2.0 * (pen_x + pen_y + pen_z)) * bottom
    applied = applied - pen_x * (x_next + x_prior)
    applied = applied - pen_y * (roll_rows(bottom, 1) + roll_rows(bottom, -1))
    applied = applied - pen_z * (has_prior * roll_lanes(bottom, 1) + has_next * roll_lanes(bottom, -1))
    rest = wb[0, 0] - applied
    change = element_product(0, [rest[b] for b in range(5)])
    for a in range(5):
        fin[40 + a] = bottom[a] + change[a]
    for n in range(45, 48):
        fin[n] = jnp.zeros((8, 128), F32)

    guess = fin[40:48]
    exchange(
        1, fin[0:48], roll_lanes(guess, EZ), roll_lanes(guess, -EZ), roll_rows(guess, 1), roll_rows(guess, -1))

    def constant_terms(tile, b, y_next, y_prior):
        py, pz = wst[tile, 102], wst[tile, 103]
        y = (py * (b - y_prior), py * (b - y_next))
        base = (wst[tile, 100] + pz) * b
        z = (base - wdg[tile, 1] * roll_lanes(b, 1), base - wdg[tile, 2] * roll_lanes(b, -1))
        return [[y[jp] + z[kp] for kp in range(2)] for jp in range(2)]

    def add_bottom(tile, b, terms, x_terms):
        for ip in range(2):
            r = []
            for a in range(5):
                own_terms = jnp.stack([terms[jp][kp][a] for jp in range(2) for kp in range(2)])
                value = w48[tile, a * 8 + ip * 4:a * 8 + ip * 4 + 4] - own_terms
                r.append(value if x_terms is None else value - x_terms[ip][a])
            for a, change in enumerate(element_product(tile, r)):
                part = pl.ds(a * 8 + ip * 4, 4)
                wm[tile, part] = wm[tile, part] + (b[a] + change)

    receive_near(1, w48, fin[0:48], 8)
    b0 = w48[0, 40:45]
    y_next = jnp.where(row == 5, wry[0:5], roll_rows(b0, -1))
    y_prior = jnp.where(row == 6, wry[0:5], roll_rows(b0, 1))
    add_bottom(0, b0, constant_terms(0, b0, y_next, y_prior), None)
    receive_far(1, w48, 48, 8)
    b1 = w48[1, 40:45]
    x_next, x_prior = across_x(b0, b1, b0, b1, wrx[0:5])
    x_terms = [
        (wst[tile, 101] * (b - x_prior[tile]), wst[tile, 101] * (b - x_next[tile]))
        for tile, b in enumerate((b0, b1))
    ]
    for ip in range(2):
        change = element_product(0, [x_terms[0][ip][a] for a in range(5)])
        for a in range(5):
            part = pl.ds(a * 8 + ip * 4, 4)
            wm[0, part] = wm[0, part] - change[a]
    add_bottom(1, b1, constant_terms(1, b1, roll_rows(b1, -1), roll_rows(b1, 1)), x_terms[1])
    for tile in range(2):
        fluxes(tile)
    middle_faces(False)
    middle_update()

    def final_parts(a, c):
        u, x, y, z, own_sides = neighbours(a, False)[0]
        wres[0, a] = wst[0, 100] * u
        for d, others in enumerate((x, y, z)):
            for side in range(2):
                p = wst[0, 101 + d]
                value = p * own_sides[d][side] - (wdg[0, 1 + side] if d == 2 else p) * others[side]
                fin[(d * 2 + side) * 20 + a * 4:(d * 2 + side) * 20 + a * 4 + 4] = value
    for a in range(5):
        final_parts(a, 0)
    fluxes(0)

    def both(value):
        return jnp.where(low_half, value, roll_rows(value, 4))

    low_a, low_b = halves(1.0, NEAR), halves(0.0, FAR)
    high_a, high_b = halves(FAR, 0.0), halves(NEAR, 1.0)

    def spread_z(v0, v1):
        return low_a * v0 + low_b * v1, high_a * v0 + high_b * v1

    def spread_line(v0, v1):
        return v0, NEAR * v0 + FAR * v1, FAR * v0 + NEAR * v1, v1

    def prolong_lines(value):
        value = both(value)
        z0, z1 = spread_z(value[:, :, 0], value[:, :, 1])
        pairs = jnp.stack([z0, z1], axis=2)
        return jnp.stack(spread_line(pairs[:, 0], pairs[:, 1]), axis=1)

    def between(lines, i):
        if i in (0, 3):
            return lines[i // 3]
        near, far = (0, 1) if i == 1 else (1, 0)
        return NEAR * lines[near] + FAR * lines[far]

    def face_lines(a, d, side):
        face = both(fin[(d * 2 + side) * 20 + a * 4:(d * 2 + side) * 20 + a * 4 + 4].reshape(2, 2, 8, 128))
        return jnp.stack(spread_z(face[:, 0], face[:, 1]), axis=1)

    def final_slabs(slabs):
        for a in range(5):
            guess, volume = lines_of[a]
            y_faces, z_faces = faces_of[a]
            for i in slabs:
                x_ref[a, i] = x_ref[a, i] + between(guess, i)
                value = res[a, i] - between(volume, i)
                if i in (0, 3):
                    z = face_lines(a, 0, i // 3)
                    value = value - jnp.stack(spread_line(z[0], z[1]))
                y = [between(face, i) for face in y_faces]
                z = jnp.stack([between(face, i) for face in z_faces], axis=1)
                value = value - z
                res[a, i] = jnp.concatenate([(value[0] - y[0])[None], value[1:3], (value[3] - y[1])[None]])

    lines_of, faces_of = [], []
    for a in range(5):
        volume = wres[0, a].reshape(2, 2, 2, 8, 128) + wc[0, 0, a].reshape(1, 2, 2, 8, 128)
        volume = volume + wc[0, 1, a].reshape(2, 1, 2, 8, 128) + wc[0, 2, a].reshape(2, 2, 1, 8, 128)
        lines_of.append((prolong_lines(wm[0, a * 8:a * 8 + 8].reshape(2, 2, 2, 8, 128)), prolong_lines(volume)))
        y_faces = [face_lines(a, 1, side) for side in range(2)]
        z_faces = []
        for side in range(2):
            face = fin[(4 + side) * 20 + a * 4:(4 + side) * 20 + a * 4 + 4].reshape(2, 2, 8, 128)
            face = lower * face if side == 0 else upper * roll_rows(face, 4)
            z_faces.append(jnp.stack(spread_line(face[:, 0], face[:, 1]), axis=1))
        faces_of.append((y_faces, z_faces))
    final_slabs((0, 3))
    for i in (0, 3):
        smooth_slab(res, i, x_ref)
    send_x_faces(2)
    final_slabs((1, 2))
    for i in (1, 2):
        smooth_slab(res, i, x_ref)
    send_y_faces(2)
    residual()
    for stage in range(2):
        for direction in range(8):
            sent(*coarse_message(stage, direction))
    for direction in range(4):
        sent(*fine_message(1, direction))
    finish_sweep(2, out_ref)
    for direction in range(4):
        sent(*fine_message(2, direction))


def solution(mesh):
    sec_count, dom_count = mesh.shape["sec"], mesh.shape["dom"]

    def on_device(defect, point_inverse, flux_jacobian, time_term, penalty, element_inverse):
        def run(*refs):
            kernel(sec_count, dom_count, *refs)

        vmem = lambda *shape: pltpu.VMEM(shape + (8, 128), F32)
        dma = lambda *shape: pltpu.SemaphoreType.DMA(shape)
        out = pl.pallas_call(
            run,
            out_shape=jax.ShapeDtypeStruct((5, 4, 4, 2, 8, 128), F32),
            in_specs=[pl.BlockSpec(memory_space=pltpu.HBM)] * 6,
            out_specs=pl.BlockSpec(memory_space=pltpu.VMEM),
            scratch_shapes=[
                vmem(5, 4, 4, 2), vmem(5, 5, 4, 4, 2), pltpu.VMEM((75, 4, 128), F32), pltpu.VMEM((4, 128), F32),
                pltpu.VMEM((3, 4, 128), F32), pltpu.VMEM((25, 4, 128), F32),
                vmem(5, 4, 4, 2), vmem(100), vmem(104), vmem(2, 4, 2), vmem(5, 4, 4, 2),
                vmem(3, 4, 5, 2), vmem(3, 4, 5, 2), vmem(4, 26), vmem(4, 26),
                vmem(2, 4, 15), vmem(2, 4, 15), vmem(2, 4, 6), vmem(2, 4, 6), vmem(4, 13), vmem(4, 13),
                vmem(2, 104), vmem(2, 3), vmem(2, 40), vmem(2, 40), vmem(2, 48), vmem(2, 5, 8), vmem(2, 3, 5, 4),
                vmem(20), vmem(20), vmem(2, 2, 5), vmem(120),
                dma(3, 4), dma(3, 4), dma(8), dma(8), dma(2, 8), dma(2, 8), dma(9),
            ],
            compiler_params=pltpu.CompilerParams(
                collective_id=0, has_side_effects=True, vmem_limit_bytes=48 << 20
            ),
        )(
            *(
                pltpu.with_memory_space_constraint(array, pltpu.HBM)
                for array in (
                    defect.reshape(5, 4, 4, 2, 8, 128),
                    point_inverse.reshape(5, 5, 4, 4, 2, 8, 128),
                    flux_jacobian.reshape(75, 4, 128),
                    time_term,
                    penalty,
                    element_inverse.reshape(25, 4, 128),
                )
            )
        )
        return out.reshape(5, 64, 4, 128)

    placed = (
        P(None, None, "sec", "dom"),
        P(None, None, None, "sec", "dom"),
        P(None, None, None, "sec", "dom"),
        P("sec", "dom"),
        P(None, "sec", "dom"),
        P(None, None, "sec", "dom"),
    )
    return jax.shard_map(
        on_device,
        mesh=mesh,
        in_specs=placed,
        out_specs=P(None, None, "sec", "dom"),
        check_vma=False,
    )
```

```python
import jax
import jax.numpy as jnp
import numpy as np
from jax import lax
from jax.experimental import pallas as pl
from jax.experimental.pallas import tpu as pltpu
from jax.sharding import PartitionSpec as P

EZ = 32
DAMPING = 0.7
MESH = pl.DeviceIdType.MESH
F32 = jnp.float32

STEPS = ((1, 0), (-1, 0), (0, 1), (0, -1), (1, 1), (1, -1), (-1, 1), (-1, -1))
RIGHT, LEFT, UP, DOWN, RIGHT_UP, RIGHT_DOWN, LEFT_UP, LEFT_DOWN = range(8)


def node_tables():
    points = np.array([-1.0, -1.0 / np.sqrt(5.0), 1.0 / np.sqrt(5.0), 1.0])
    barycentric = np.array(
        [1.0 / np.prod([points[j] - points[k] for k in range(4) if k != j]) for j in range(4)]
    )
    derivative = np.zeros((4, 4))
    for i in range(4):
        for j in range(4):
            if i != j:
                derivative[i, j] = barycentric[j] / barycentric[i] / (points[i] - points[j])
        derivative[i, i] = -np.sum(derivative[i])
    return derivative, (1.0 - points[1]) / 2.0, (1.0 + points[1]) / 2.0


DERIVATIVE, NEAR, FAR = node_tables()
EVEN = [float((DERIVATIVE[i, 0] + DERIVATIVE[i, 3]) / 2.0) for i in (0, 1)]
ODD = [[float((DERIVATIVE[i, j] - DERIVATIVE[i, 3 - j]) / 2.0) for j in (0, 1)] for i in (0, 1)]
NEAR, FAR = float(NEAR), float(FAR)


def roll_lanes(value, shift):
    shift %= 128
    return value if shift == 0 else pltpu.roll(value, shift, value.ndim - 1)


def roll_rows(value, shift):
    shift %= 8
    return value if shift == 0 else pltpu.roll(value, shift, value.ndim - 2)


def repeat(count, body):
    for n in range(count):
        body(n, 0)


def kernel(
    sec_count, dom_count,
    s_hbm, b_hbm, j_hbm, t_hbm, p_hbm, e_hbm,
    out_ref,
    s_ref, b_ref, j_ref, t_ref, p_ref, e_ref,
    x_ref, jd, own, dg, res,
    fsend, frecv, ssend, srecv, esend, erecv, dsend, drecv, dssend, dsrecv,
    wst, wdg, wm, ws, w48, wres, wc, wrx, wry, wb, fin,
    f_ss, f_rs, s_ss, s_rs, e_ss, e_rs, in_sem,
):
    small = [
        pltpu.make_async_copy(source, kept, in_sem.at[4 + n])
        for n, (source, kept) in enumerate(
            ((s_hbm, s_ref), (j_hbm, j_ref), (e_hbm, e_ref), (t_hbm, t_ref), (p_hbm, p_ref)))
    ]
    blocks = [
        pltpu.make_async_copy(b_hbm.at[:, :, i], b_ref.at[:, :, i], in_sem.at[i]) for i in range(4)
    ]
    for transfer in [small[0], blocks[0], blocks[3], blocks[1], blocks[2]] + small[1:]:
        transfer.start()
    me_sec, me_dom = lax.axis_index("sec"), lax.axis_index("dom")
    has_dom = {0: None, 1: me_dom < dom_count - 1, -1: me_dom > 0}
    has_sec = {0: None, 1: me_sec < sec_count - 1, -1: me_sec > 0}

    def exists(dx, dy):
        a, b = has_dom[dx], has_sec[dy]
        if a is None:
            return b
        if b is None:
            return a
        return jnp.logical_and(a, b)

    def target(direction):
        dx, dy = STEPS[direction]
        return (me_sec + dy, me_dom + dx)

    barrier = pltpu.get_barrier_semaphore()
    for direction in range(8):
        @pl.when(exists(*STEPS[direction]))
        def _(direction=direction):
            pl.semaphore_signal(barrier, inc=1, device_id=target(direction), device_id_type=MESH)
    one, zero = jnp.int32(1), jnp.int32(0)
    across = jnp.where(me_dom < dom_count - 1, one, zero) + jnp.where(me_dom > 0, one, zero) + 1
    along = jnp.where(me_sec < sec_count - 1, one, zero) + jnp.where(me_sec > 0, one, zero) + 1

    def copy(direction, src, dst, send_sem, recv_sem):
        return pltpu.make_async_remote_copy(
            src_ref=src, dst_ref=dst, send_sem=send_sem, recv_sem=recv_sem,
            device_id=target(direction), device_id_type=MESH,
        )

    def send(direction, src, dst, send_sem, recv_sem):
        @pl.when(exists(*STEPS[direction]))
        def _():
            copy(direction, src, dst, send_sem, recv_sem).start()

    def sent(direction, src, dst, send_sem, recv_sem):
        @pl.when(exists(*STEPS[direction]))
        def _():
            copy(direction, src, dst, send_sem, recv_sem).wait_send()

    def arrived(direction, src, dst, send_sem, recv_sem):
        dx, dy = STEPS[direction]

        @pl.when(exists(-dx, -dy))
        def _():
            copy(direction, src, dst, send_sem, recv_sem).wait_recv()

    def clear(direction, dst):
        dx, dy = STEPS[direction]

        @pl.when(jnp.logical_not(exists(-dx, -dy)))
        def _():
            dst[...] = jnp.zeros_like(dst)

    def fine_message(stage, direction):
        return (direction, fsend.at[stage, direction], frecv.at[stage, direction],
                f_ss.at[stage, direction], f_rs.at[stage, direction])

    def static_message(direction):
        if direction < 4:
            src, dst = ssend.at[direction], srecv.at[direction]
        else:
            src, dst = dssend.at[direction - 4], dsrecv.at[direction - 4]
        return direction, src, dst, s_ss.at[direction], s_rs.at[direction]

    def coarse_message(stage, direction):
        if direction < 4:
            part = pl.ds(0, (15, 14)[stage])
            src, dst = esend.at[stage, direction, part], erecv.at[stage, direction, part]
        else:
            part = pl.ds(0, (5, 6)[stage])
            src, dst = dsend.at[stage, direction - 4, part], drecv.at[stage, direction - 4, part]
        return direction, src, dst, e_ss.at[stage, direction], e_rs.at[stage, direction]

    lane = lax.broadcasted_iota(jnp.int32, (8, 128), 1)
    row = lax.broadcasted_iota(jnp.int32, (8, 128), 0)
    low_half = row < 4
    low_lanes = lane < 64
    z_index = lane % EZ
    has_next = jnp.where(z_index < EZ - 1, 1.0, 0.0)
    has_prior = jnp.where(z_index > 0, 1.0, 0.0)
    lower = jnp.where(low_half, 1.0, 0.0)
    upper = 1.0 - lower
    row4 = row % 4

    def halves(a, b):
        return jnp.where(low_half, F32(a), F32(b))

    def smooth(source, i, j, target, first):
        part = pl.ds(j, 2)
        values = [source[a, i, part] for a in range(5)]
        totals = []
        for a in range(5):
            total = b_ref[a, 0, i, part] * values[0]
            for b in range(1, 5):
                total = total + b_ref[a, b, i, part] * values[b]
            total = DAMPING * total
            totals.append(total if first else x_ref[a, i, part] + total)
        for a in range(5):
            target[a, i, part] = totals[a]

    def smooth_slab(source, i, target, first=False):
        for j in (0, 2):
            smooth(source, i, j, target, first)

    def pieces(face, rolled, place):
        packed = None
        for m in range(4):
            piece = rolled(face(m), m)
            packed = piece if packed is None else jnp.where(place == m, piece, packed)
        return packed

    def send_x_faces(stage):
        fsend[stage, RIGHT] = pieces(
            lambda m: x_ref[:, 3, m], lambda v, m: roll_lanes(v, EZ * (m + 1)), lane // EZ)
        fsend[stage, LEFT] = pieces(
            lambda m: x_ref[:, 0, m], lambda v, m: roll_lanes(v, EZ * m), lane // EZ)
        for direction in (RIGHT, LEFT):
            send(*fine_message(stage, direction))

    def send_y_faces(stage):
        fsend[stage, UP] = pieces(
            lambda m: x_ref[:, m, 3], lambda v, m: roll_rows(v, m - 3), row4)
        fsend[stage, DOWN] = pieces(
            lambda m: x_ref[:, m, 0], lambda v, m: roll_rows(v, m), row4)
        for direction in (UP, DOWN):
            send(*fine_message(stage, direction))

    even_z = halves(EVEN[0], EVEN[1])
    even_z_swapped = halves(EVEN[1], EVEN[0])
    odd_z = halves(ODD[0][0], ODD[1][1])
    odd_z_cross = halves(ODD[0][1], ODD[1][0])
    odd_z_swapped = halves(ODD[1][1], ODD[0][0])
    odd_z_cross_swapped = halves(ODD[1][0], ODD[0][1])

    def jacobian(d, parts):
        out = []
        for a in range(5):
            total = [jd[d * 25 + a * 5] * value for value in parts[0]]
            for b in range(1, 5):
                block = jd[d * 25 + a * 5 + b]
                total = [t + block * value for t, value in zip(total, parts[b])]
            out.append(total)
        return out

    def line_parts(u):
        return [u[0] - u[3], u[1] - u[2], (u[0] + u[3]) - (u[1] + u[2])]

    def line_slopes(outer, inner, even):
        e0, e1 = EVEN[0] * even, EVEN[1] * even
        o0 = ODD[0][0] * outer + ODD[0][1] * inner
        o1 = ODD[1][0] * outer + ODD[1][1] * inner
        return o0 + e0, o1 + e1, o1 - e1, o0 - e0

    def residual():
        def along_x(n, c):
            j, k2 = n // 2, n % 2
            inner_weight, outer_weight = dg[0, j, k2], dg[1, j, k2]
            u = [x_ref[a, :, j, k2] for a in range(5)]
            flux = jacobian(0, [line_parts(v) for v in u])
            out = []
            for a in range(5):
                slopes = line_slopes(*flux[a])
                s = s_ref[a, :, j, k2]
                v = u[a]
                out.append(jnp.stack([
                    (s[0] - outer_weight * v[0]) + (px_prior * roll_lanes(v[3], EZ) - slopes[0]),
                    (s[1] - inner_weight * v[1]) - slopes[1],
                    (s[2] - inner_weight * v[2]) - slopes[2],
                    (s[3] - outer_weight * v[3]) + (px_next * roll_lanes(v[0], -EZ) - slopes[3]),
                ]))
            for a in range(5):
                res[a, :, j, k2] = out[a]
            return c
        repeat(8, along_x)

        def along_y(n, c):
            i, k2 = n // 2, n % 2
            u = [x_ref[a, i, :, k2] for a in range(5)]
            flux = jacobian(1, [line_parts(v) for v in u])
            out = []
            for a in range(5):
                slopes = line_slopes(*flux[a])
                r = res[a, i, :, k2]
                v = u[a]
                out.append(jnp.stack([
                    r[0] + (py_prior * roll_rows(v[3], 1) - slopes[0]),
                    r[1] - slopes[1],
                    r[2] - slopes[2],
                    r[3] + (py_next * roll_rows(v[0], -1) - slopes[3]),
                ]))
            for a in range(5):
                res[a, i, :, k2] = out[a]
            return c
        repeat(8, along_y)

        def along_z(n, c):
            i, j = n // 2, 2 * (n % 2)
            part = pl.ds(j, 2)
            parts, adds = [], []
            for a in range(5):
                u = x_ref[a, i, part]
                v0, v1 = u[:, 0], u[:, 1]
                w0, w1 = roll_rows(v0, 4), roll_rows(v1, 4)
                straight, swapped = v0 + w1, w0 + v1
                odd = v0 - w1
                even = jnp.where(low_half, straight[0] - swapped[0], swapped[1] - straight[1])
                parts.append([odd[0], odd[1], even])
                adds.append(jnp.stack([pz_prior * roll_lanes(w1, 1), pz_next * roll_lanes(w0, -1)], axis=1))
            flux = jacobian(2, parts)
            out = []
            for a in range(5):
                turned = roll_rows(flux[a][2], 4)
                even = (jnp.where(low_half, flux[a][2], turned), jnp.where(low_half, turned, flux[a][2]))
                lines = []
                for m in range(2):
                    odd = flux[a][m]
                    cross = roll_rows(odd, 4)
                    lines.append(jnp.stack([
                        odd_z * odd + odd_z_cross * cross + even_z * even[m],
                        odd_z_swapped * cross + odd_z_cross_swapped * odd - even_z_swapped * even[m],
                    ]))
                out.append(res[a, i, part] + (adds[a] - jnp.stack(lines)))
            for a in range(5):
                res[a, i, part] = out[a]
            return c
        repeat(8, along_z)

    def add_y_halo(stage):
        for direction in (UP, DOWN):
            arrived(*fine_message(stage, direction))
        from_below, from_above = frecv[stage, UP], frecv[stage, DOWN]
        for m in range(4):
            res[:, m, 0] = res[:, m, 0] + py_below * roll_rows(from_below, -m)
            res[:, m, 3] = res[:, m, 3] + py_above * roll_rows(from_above, 3 - m)

    def add_x_halo(stage):
        for direction in (RIGHT, LEFT):
            arrived(*fine_message(stage, direction))
        from_left, from_right = frecv[stage, RIGHT], frecv[stage, LEFT]
        for m in range(4):
            res[:, 0, m] = res[:, 0, m] + px_left * roll_lanes(from_left, -EZ * m)
            res[:, 3, m] = res[:, 3, m] + px_right * roll_lanes(from_right, 128 - EZ * (m + 1))

    def finish_sweep(stage, target):
        add_y_halo(stage)
        for i in (1, 2):
            smooth_slab(res, i, target)
        add_x_halo(stage)
        for i in (0, 3):
            smooth_slab(res, i, target)

    def pack_columns(value, first_block):
        quarter = value.shape[0] // 4
        packed = None
        for m in range(4):
            piece = roll_rows(roll_lanes(value[m * quarter:(m + 1) * quarter], 64 * (m % 2)), 4 * (m // 2))
            place = jnp.logical_and(row // 4 == m // 2, lane // 64 == (first_block + m) % 2)
            packed = piece if packed is None else jnp.where(place, piece, packed)
        return packed

    def pack_rows(value, first_pair):
        quarter = value.shape[0] // 4
        packed = None
        for m in range(4):
            piece = roll_rows(value[m * quarter:(m + 1) * quarter], 2 * m)
            packed = piece if packed is None else jnp.where(row // 2 == (first_pair + m) % 4, piece, packed)
        return packed

    def pack_corner(rows_packed, keep_low):
        half = rows_packed.shape[0] // 2
        return jnp.where(low_lanes == keep_low, rows_packed[:half], roll_lanes(rows_packed[half:], 64))

    def unpack_columns(from_right, from_left):
        out = []
        for m in range(4):
            both = jnp.where(lane // 64 == m % 2, from_right, from_left)
            out.append(roll_rows(roll_lanes(both, -64 * (m % 2)), -4 * (m // 2)))
        return out

    def unpack_rows(from_above, from_below):
        return [roll_rows(jnp.where(row // 2 == m, from_above, from_below), 4 - 2 * m) for m in range(4)]

    def unpack_corner(right, left):
        return jnp.concatenate(
            [jnp.where(low_lanes, right, left), roll_lanes(jnp.where(low_lanes, left, right), 64)], axis=0)

    def fill_near(window, mine, rows):
        quarter = mine.shape[0] // 4
        ends = unpack_rows(rows[0], rows[1])
        for m in range(4):
            part = slice(m * quarter, (m + 1) * quarter)
            window[0, part] = jnp.where(low_half, mine[part], ends[m])

    def fill_far(window, columns, corners):
        quarter = columns[0].shape[0]
        side = unpack_columns(columns[0], columns[1])
        above = unpack_corner(corners[0], corners[1])
        below = unpack_corner(corners[2], corners[3])
        edge = unpack_rows(above, below)
        for m in range(4):
            window[1, m * quarter:(m + 1) * quarter] = jnp.where(low_half, side[m], edge[m])

    small[0].wait()
    for i in (0, 3):
        blocks[i].wait()
        smooth_slab(s_ref, i, x_ref, True)
    pl.semaphore_wait(barrier, across * along - 1)
    send_x_faces(0)
    for i in (1, 2):
        blocks[i].wait()
        smooth_slab(s_ref, i, x_ref, True)
    send_y_faces(0)

    for transfer in small[1:]:
        transfer.wait()
    for array, start, count, scale in ((j_ref, 0, 75, 0.5), (e_ref, 75, 25, DAMPING)):
        value = array[...]
        jd[start:start + count, 0:4] = value
        jd[start:start + count, 4:8] = value
    own[0:75] = 0.5 * jd[0:75]
    own[75:100] = DAMPING * jd[75:100]
    for n, value in enumerate((t_ref[...], p_ref[0], p_ref[1], p_ref[2])):
        own[100 + n, 0:4] = value
        own[100 + n, 4:8] = value
    time, pen_x, pen_y, pen_z = own[100], own[101], own[102], own[103]
    for f in range(2):
        for j in range(4):
            for k2 in range(2):
                total = time + pen_z * (lower if k2 == 0 else upper)
                if j in (0, 3):
                    total = total + pen_y
                dg[f, j, k2] = total + pen_x if f else total

    px_prior = jnp.where(lane >= EZ, pen_x, 0.0)
    px_next = jnp.where(lane < 128 - EZ, pen_x, 0.0)
    px_left = jnp.where(lane < EZ, pen_x, 0.0)
    px_right = jnp.where(lane >= 128 - EZ, pen_x, 0.0)
    py_prior = jnp.where(row4 != 0, pen_y, 0.0)
    py_next = jnp.where(row4 != 3, pen_y, 0.0)
    py_below = jnp.where(row4 == 0, pen_y, 0.0)
    py_above = jnp.where(row4 == 3, pen_y, 0.0)
    pz_prior = pen_z * lower * has_prior
    pz_next = pen_z * upper * has_next

    coefficients = own[...]
    ssend[RIGHT] = pack_columns(coefficients, 1)
    ssend[LEFT] = pack_columns(coefficients, 0)
    ssend[UP] = pack_rows(coefficients, 1)
    ssend[DOWN] = pack_rows(coefficients, 0)
    for direction, source, keep_low in (
        (RIGHT_UP, UP, False), (RIGHT_DOWN, DOWN, False), (LEFT_UP, UP, True), (LEFT_DOWN, DOWN, True)
    ):
        dssend[direction - 4] = pack_corner(ssend[source], keep_low)
    for direction in range(8):
        send(*static_message(direction))
    for stage in range(3):
        for direction in range(4):
            clear(direction, frecv.at[stage, direction])
    for stage in range(2):
        for direction in range(4):
            clear(direction, erecv.at[stage, direction])
        for direction in range(4, 8):
            clear(direction, drecv.at[stage, direction - 4])
    for direction in range(4):
        clear(direction, srecv.at[direction])
    for direction in range(4, 8):
        clear(direction, dsrecv.at[direction - 4])

    residual()
    finish_sweep(0, x_ref)
    send_x_faces(1)
    send_y_faces(1)
    residual()
    for direction in range(4):
        sent(*fine_message(0, direction))
    for direction in range(8):
        sent(*static_message(direction))
    for direction in range(8):
        arrived(*static_message(direction))
    fill_near(wst, own, (srecv[DOWN], srecv[UP]))
    fill_far(
        wst, (srecv[LEFT], srecv[RIGHT]),
        (dsrecv[LEFT_DOWN - 4], dsrecv[RIGHT_DOWN - 4], dsrecv[LEFT_UP - 4], dsrecv[RIGHT_UP - 4]),
    )
    for tile in range(2):
        px, py, pz = wst[tile, 101], wst[tile, 102], wst[tile, 103]
        wdg[tile, 0] = wst[tile, 100] + (px + py + pz)
        wdg[tile, 1] = pz * has_prior
        wdg[tile, 2] = pz * has_next
    add_y_halo(1)
    add_x_halo(1)

    near_low, far_low = halves(1.0, NEAR), halves(FAR, 0.0)
    near_high, far_high = halves(NEAR, 1.0), halves(0.0, FAR)

    for a in range(5):
        for ip in range(2):
            if ip == 0:
                x = res[a, 0] + NEAR * res[a, 1] + FAR * res[a, 2]
            else:
                x = FAR * res[a, 1] + NEAR * res[a, 2] + res[a, 3]
            for jp in range(2):
                if jp == 0:
                    y = x[0] + NEAR * x[1] + FAR * x[2]
                else:
                    y = FAR * x[1] + NEAR * x[2] + x[3]
                z0 = near_low * y[0] + far_low * y[1]
                z1 = far_high * y[0] + near_high * y[1]
                n = a * 8 + ip * 4 + jp * 2
                fin[n] = z0 + roll_rows(z0, 4)
                fin[n + 1] = z1 + roll_rows(z1, 4)

    CORNERS = ((RIGHT_UP, UP, False), (RIGHT_DOWN, DOWN, False), (LEFT_UP, UP, True), (LEFT_DOWN, DOWN, True))

    def exchange(stage, field, strips):
        main = field.shape[0] // 4
        esend[stage, UP, 0:main] = pack_rows(field, 1)
        esend[stage, DOWN, 0:main] = pack_rows(field, 0)
        for direction, source, keep_low in CORNERS:
            dsend[stage, direction - 4, 0:main // 2] = pack_corner(esend[stage, source, 0:main], keep_low)
        for direction, _, _ in CORNERS:
            send(*coarse_message(stage, direction))
        x_prior, x_next, y_prior, y_next = strips()
        whole = main + x_prior.shape[0] // 4
        esend[stage, RIGHT, 0:main] = pack_columns(field, 1)
        esend[stage, RIGHT, main:whole] = pack_columns(x_prior, 1)
        esend[stage, LEFT, 0:main] = pack_columns(field, 0)
        esend[stage, LEFT, main:whole] = pack_columns(x_next, 0)
        for direction in (RIGHT, LEFT):
            send(*coarse_message(stage, direction))
        esend[stage, UP, main:whole] = pack_rows(y_prior, 1)
        esend[stage, DOWN, main:whole] = pack_rows(y_next, 0)
        for direction in (UP, DOWN):
            send(*coarse_message(stage, direction))

    def receive_near(stage, window, field, strips):
        main, more = field.shape[0] // 4, strips // 4
        for direction in (UP, DOWN):
            arrived(*coarse_message(stage, direction))
        fill_near(window, field, (erecv[stage, DOWN, 0:main], erecv[stage, UP, 0:main]))
        ends = unpack_rows(erecv[stage, DOWN, main:main + more], erecv[stage, UP, main:main + more])
        for m in range(4):
            wry[more * m:more * m + more] = ends[m]

    def receive_far(stage, window, fields, strips):
        main, more = fields // 4, strips // 4
        for direction in (RIGHT, LEFT, RIGHT_UP, RIGHT_DOWN, LEFT_UP, LEFT_DOWN):
            arrived(*coarse_message(stage, direction))
        half = main // 2
        fill_far(
            window, (erecv[stage, LEFT, 0:main], erecv[stage, RIGHT, 0:main]),
            (drecv[stage, LEFT_DOWN - 4, 0:half], drecv[stage, RIGHT_DOWN - 4, 0:half],
             drecv[stage, LEFT_UP - 4, 0:half], drecv[stage, RIGHT_UP - 4, 0:half]),
        )
        side = unpack_columns(erecv[stage, LEFT, main:main + more], erecv[stage, RIGHT, main:main + more])
        for m in range(4):
            wrx[more * m:more * m + more] = side[m]

    strip_right = jnp.logical_and(low_half, lane // EZ == 1)
    strip_left = jnp.logical_and(low_half, lane // EZ == 2)

    def across_x(low0, low1, up0, up1, strip):
        l0, l1 = roll_lanes(low0, -EZ), roll_lanes(low1, -EZ)
        u0, u1 = roll_lanes(up0, EZ), roll_lanes(up1, EZ)
        not_last, first = lane < 128 - EZ, lane < EZ
        next0, next1 = jnp.where(not_last, l0, l1), jnp.where(not_last, l1, l0)
        prior0, prior1 = jnp.where(first, u1, u0), jnp.where(first, u0, u1)
        if strip is not None:
            next1 = jnp.where(strip_right, strip, next1)
            prior1 = jnp.where(strip_left, strip, prior1)
        return (next0, next1), (prior0, prior1)

    def neighbours(a, use_strips):
        tiles = [wm[tile, a * 8:a * 8 + 8] for tile in range(2)]
        nodes = [u.reshape(2, 2, 2, 8, 128) for u in tiles]
        x_low, x_up = [u[0].reshape(4, 8, 128) for u in nodes], [u[1].reshape(4, 8, 128) for u in nodes]
        y_low, y_up = [u[:, 0].reshape(4, 8, 128) for u in nodes], [u[:, 1].reshape(4, 8, 128) for u in nodes]
        z_low, z_up = [u[:, :, 0].reshape(4, 8, 128) for u in nodes], [u[:, :, 1].reshape(4, 8, 128) for u in nodes]
        x_next, x_prior = across_x(
            x_low[0], x_low[1], x_up[0], x_up[1], wrx[a * 4:a * 4 + 4] if use_strips else None)
        out = []
        for tile in range(2):
            y_next, y_prior = roll_rows(y_low[tile], -1), roll_rows(y_up[tile], 1)
            if tile == 0 and use_strips:
                strip = wry[a * 4:a * 4 + 4]
                y_next = jnp.where(row == 5, strip, y_next)
                y_prior = jnp.where(row == 6, strip, y_prior)
            out.append((
                tiles[tile], (x_prior[tile], x_next[tile]), (y_prior, y_next),
                (roll_lanes(z_up[tile], 1), roll_lanes(z_low[tile], -1)),
                ((x_low[tile], x_up[tile]), (y_low[tile], y_up[tile]), (z_low[tile], z_up[tile])),
            ))
        return out

    def fluxes(tile):
        slopes = ([], [], [])
        for a in range(5):
            u = wm[tile, a * 8:a * 8 + 8].reshape(2, 2, 2, 8, 128)
            slopes[0].append((u[1] - u[0]).reshape(4, 8, 128))
            slopes[1].append((u[:, 1] - u[:, 0]).reshape(4, 8, 128))
            slopes[2].append((u[:, :, 1] - u[:, :, 0]).reshape(4, 8, 128))
        for d in range(3):
            for a in range(5):
                total = wst[tile, d * 25 + a * 5] * slopes[d][0]
                for b in range(1, 5):
                    total = total + wst[tile, d * 25 + a * 5 + b] * slopes[d][b]
                wc[tile, d, a] = total

    def middle_faces(use_strips, tiles=2):
        for a in range(5):
            for tile, (u, x, y, z, _) in enumerate(neighbours(a, use_strips)[:tiles]):
                px, py = wst[tile, 101], wst[tile, 102]
                pz = (wdg[tile, 1], wdg[tile, 2])
                r = (ws[tile, a * 8:a * 8 + 8] - wdg[tile, 0] * u).reshape(2, 2, 2, 8, 128)
                r = r + jnp.stack([px * v for v in x], axis=0).reshape(2, 2, 2, 8, 128)
                r = r + jnp.stack([(py * v).reshape(2, 2, 8, 128) for v in y], axis=1)
                r = r + jnp.stack([(p * v).reshape(2, 2, 8, 128) for p, v in zip(pz, z)], axis=2)
                wres[tile, a] = r.reshape(8, 8, 128)

    def full_residual(tile, ip, a):
        r = wres[tile, a, pl.ds(ip * 4, 4)].reshape(2, 2, 8, 128)
        r = r - wc[tile, 0, a].reshape(2, 2, 8, 128)
        r = r - wc[tile, 1, a, pl.ds(ip * 2, 2)][None]
        return r - wc[tile, 2, a, pl.ds(ip * 2, 2)][:, None]

    def element_product(tile, values):
        out = []
        for a in range(5):
            total = wst[tile, 75 + a * 5] * values[0]
            for b in range(1, 5):
                total = total + wst[tile, 75 + a * 5 + b] * values[b]
            out.append(total)
        return out

    def middle_update():
        for tile in range(2):
            for ip in range(2):
                r = [full_residual(tile, ip, a).reshape(4, 8, 128) for a in range(5)]
                parts = [pl.ds(a * 8 + ip * 4, 4) for a in range(5)]
                for part, change in zip(parts, element_product(tile, r)):
                    wm[tile, part] = wm[tile, part] + change

    def first_guess(tile):
        for ip in range(2):
            part = [ws[tile, pl.ds(b * 8 + ip * 4, 4)] for b in range(5)]
            for a, value in enumerate(element_product(tile, part)):
                wm[tile, pl.ds(a * 8 + ip * 4, 4)] = value

    def own_strips():
        for ip in range(2):
            part = [fin[pl.ds(b * 8 + ip * 4, 4)] for b in range(5)]
            for a, value in enumerate(element_product(0, part)):
                fin[pl.ds(40 + a * 8 + ip * 4, 4)] = value
        nodes = fin[40:80].reshape(5, 2, 2, 2, 8, 128)
        return (
            roll_lanes(nodes[:, 1].reshape(20, 8, 128), EZ), roll_lanes(nodes[:, 0].reshape(20, 8, 128), -EZ),
            roll_rows(nodes[:, :, 1].reshape(20, 8, 128), 1), roll_rows(nodes[:, :, 0].reshape(20, 8, 128), -1),
        )
    exchange(0, fin[0:40], own_strips)
    receive_near(0, ws, fin[0:40], 20)
    first_guess(0)
    fluxes(0)
    receive_far(0, ws, 40, 20)
    first_guess(1)
    fluxes(1)
    middle_faces(True)
    middle_update()
    fluxes(0)
    middle_faces(False, 1)

    def far_sources():
        rest, slopes = [], ([], [], [])
        for a in range(5):
            u = wm[1, a * 8:a * 8 + 8].reshape(2, 2, 2, 8, 128)
            v = wm[0, a * 8:a * 8 + 8].reshape(2, 4, 8, 128)
            pairs = u[:, :, 0] + u[:, :, 1]
            x_low, x_up = pairs[0, 0] + pairs[0, 1], pairs[1, 0] + pairs[1, 1]
            y_low, y_up = pairs[0, 0] + pairs[1, 0], pairs[0, 1] + pairs[1, 1]
            z = u[0] + u[1]
            z_low, z_up = z[0, 0] + z[1, 0], z[0, 1] + z[1, 1]
            near_low = (v[0, 0] + v[0, 1]) + (v[0, 2] + v[0, 3])
            near_up = (v[1, 0] + v[1, 1]) + (v[1, 2] + v[1, 3])
            (_, x_next), (_, x_prior) = across_x(near_low, x_low, near_up, x_up, None)
            total = ws[1, a * 8]
            for n in range(1, 8):
                total = total + ws[1, a * 8 + n]
            total = total - wdg[1, 0] * (x_low + x_up)
            total = total + wst[1, 101] * (x_next + x_prior)
            total = total + wst[1, 102] * (roll_rows(y_low, -1) + roll_rows(y_up, 1))
            total = total + (wdg[1, 1] * roll_lanes(z_up, 1) + wdg[1, 2] * roll_lanes(z_low, -1))
            rest.append(total)
            for d, slope in enumerate((x_up - x_low, y_up - y_low, z_up - z_low)):
                slopes[d].append(2.0 * slope)
        for a in range(5):
            for d in range(3):
                for b in range(5):
                    rest[a] = rest[a] - wst[1, d * 25 + a * 5 + b] * slopes[d][b]
        return rest

    def near_sources():
        source = []
        for a in range(5):
            parts = [full_residual(0, ip, a) for ip in range(2)]
            for ip in range(2):
                fin[a * 8 + ip * 4:a * 8 + ip * 4 + 4] = parts[ip].reshape(4, 8, 128)
            total = parts[0] + parts[1]
            total = total[0] + total[1]
            source.append(total[0] + total[1])
        return source

    for tile, source in enumerate((near_sources(), far_sources())):
        for a in range(5):
            wb[0, tile, a] = source[a]
        for a, value in enumerate(element_product(tile, source)):
            wb[1, tile, a] = value
    bottom = wb[1, 0]
    (x_next, _), (x_prior, _) = across_x(bottom, wb[1, 1], bottom, wb[1, 1], None)
    applied = (time + 2.0 * (pen_x + pen_y + pen_z)) * bottom
    applied = applied - pen_x * (x_next + x_prior)
    applied = applied - pen_y * (roll_rows(bottom, 1) + roll_rows(bottom, -1))
    applied = applied - pen_z * (has_prior * roll_lanes(bottom, 1) + has_next * roll_lanes(bottom, -1))
    rest = wb[0, 0] - applied
    change = element_product(0, [rest[b] for b in range(5)])
    for a in range(5):
        fin[40 + a] = bottom[a] + change[a]
    for n in range(45, 48):
        fin[n] = jnp.zeros((8, 128), F32)

    guess = fin[40:48]
    exchange(
        1, fin[0:48],
        lambda: (roll_lanes(guess, EZ), roll_lanes(guess, -EZ), roll_rows(guess, 1), roll_rows(guess, -1)))

    def constant_terms(tile, b, y_next, y_prior):
        py, pz = wst[tile, 102], wst[tile, 103]
        y = (py * (b - y_prior), py * (b - y_next))
        base = (wst[tile, 100] + pz) * b
        z = (base - wdg[tile, 1] * roll_lanes(b, 1), base - wdg[tile, 2] * roll_lanes(b, -1))
        return [[y[jp] + z[kp] for kp in range(2)] for jp in range(2)]

    def add_bottom(tile, b, terms, x_terms):
        for ip in range(2):
            r = []
            for a in range(5):
                own_terms = jnp.stack([terms[jp][kp][a] for jp in range(2) for kp in range(2)])
                value = w48[tile, a * 8 + ip * 4:a * 8 + ip * 4 + 4] - own_terms
                r.append(value if x_terms is None else value - x_terms[ip][a])
            for a, change in enumerate(element_product(tile, r)):
                part = pl.ds(a * 8 + ip * 4, 4)
                wm[tile, part] = wm[tile, part] + (b[a] + change)

    receive_near(1, w48, fin[0:48], 8)
    b0 = w48[0, 40:45]
    y_next = jnp.where(row == 5, wry[0:5], roll_rows(b0, -1))
    y_prior = jnp.where(row == 6, wry[0:5], roll_rows(b0, 1))
    add_bottom(0, b0, constant_terms(0, b0, y_next, y_prior), None)
    receive_far(1, w48, 48, 8)
    b1 = w48[1, 40:45]
    x_next, x_prior = across_x(b0, b1, b0, b1, wrx[0:5])
    x_terms = [
        (wst[tile, 101] * (b - x_prior[tile]), wst[tile, 101] * (b - x_next[tile]))
        for tile, b in enumerate((b0, b1))
    ]
    for ip in range(2):
        change = element_product(0, [x_terms[0][ip][a] for a in range(5)])
        for a in range(5):
            part = pl.ds(a * 8 + ip * 4, 4)
            wm[0, part] = wm[0, part] - change[a]
    add_bottom(1, b1, constant_terms(1, b1, roll_rows(b1, -1), roll_rows(b1, 1)), x_terms[1])
    for tile in range(2):
        fluxes(tile)
    middle_faces(False)
    middle_update()

    def final_parts(a, c):
        u, x, y, z, own_sides = neighbours(a, False)[0]
        wres[0, a] = wst[0, 100] * u
        for d, others in enumerate((x, y, z)):
            for side in range(2):
                p = wst[0, 101 + d]
                value = p * own_sides[d][side] - (wdg[0, 1 + side] if d == 2 else p) * others[side]
                fin[(d * 2 + side) * 20 + a * 4:(d * 2 + side) * 20 + a * 4 + 4] = value
    for a in range(5):
        final_parts(a, 0)
    fluxes(0)

    def both(value):
        return jnp.where(low_half, value, roll_rows(value, 4))

    low_a, low_b = halves(1.0, NEAR), halves(0.0, FAR)
    high_a, high_b = halves(FAR, 0.0), halves(NEAR, 1.0)

    def spread_z(v0, v1):
        return low_a * v0 + low_b * v1, high_a * v0 + high_b * v1

    def spread_line(v0, v1):
        return v0, NEAR * v0 + FAR * v1, FAR * v0 + NEAR * v1, v1

    def prolong_lines(value):
        value = both(value)
        z0, z1 = spread_z(value[:, :, 0], value[:, :, 1])
        pairs = jnp.stack([z0, z1], axis=2)
        return jnp.stack(spread_line(pairs[:, 0], pairs[:, 1]), axis=1)

    def between(lines, i):
        if i in (0, 3):
            return lines[i // 3]
        near, far = (0, 1) if i == 1 else (1, 0)
        return NEAR * lines[near] + FAR * lines[far]

    def face_lines(a, d, side):
        face = both(fin[(d * 2 + side) * 20 + a * 4:(d * 2 + side) * 20 + a * 4 + 4].reshape(2, 2, 8, 128))
        return jnp.stack(spread_z(face[:, 0], face[:, 1]), axis=1)

    def final_slabs(slabs):
        for a in range(5):
            guess, volume = lines_of[a]
            y_faces, z_faces = faces_of[a]
            for i in slabs:
                x_ref[a, i] = x_ref[a, i] + between(guess, i)
                value = res[a, i] - between(volume, i)
                if i in (0, 3):
                    z = face_lines(a, 0, i // 3)
                    value = value - jnp.stack(spread_line(z[0], z[1]))
                y = [between(face, i) for face in y_faces]
                z = jnp.stack([between(face, i) for face in z_faces], axis=1)
                value = value - z
                res[a, i] = jnp.concatenate([(value[0] - y[0])[None], value[1:3], (value[3] - y[1])[None]])

    lines_of, faces_of = [], []
    for a in range(5):
        volume = wres[0, a].reshape(2, 2, 2, 8, 128) + wc[0, 0, a].reshape(1, 2, 2, 8, 128)
        volume = volume + wc[0, 1, a].reshape(2, 1, 2, 8, 128) + wc[0, 2, a].reshape(2, 2, 1, 8, 128)
        lines_of.append((prolong_lines(wm[0, a * 8:a * 8 + 8].reshape(2, 2, 2, 8, 128)), prolong_lines(volume)))
        y_faces = [face_lines(a, 1, side) for side in range(2)]
        z_faces = []
        for side in range(2):
            face = fin[(4 + side) * 20 + a * 4:(4 + side) * 20 + a * 4 + 4].reshape(2, 2, 8, 128)
            face = lower * face if side == 0 else upper * roll_rows(face, 4)
            z_faces.append(jnp.stack(spread_line(face[:, 0], face[:, 1]), axis=1))
        faces_of.append((y_faces, z_faces))
    final_slabs((0, 3))
    for i in (0, 3):
        smooth_slab(res, i, x_ref)
    send_x_faces(2)
    final_slabs((1, 2))
    for i in (1, 2):
        smooth_slab(res, i, x_ref)
    send_y_faces(2)
    residual()
    for stage in range(2):
        for direction in range(8):
            sent(*coarse_message(stage, direction))
    for direction in range(4):
        sent(*fine_message(1, direction))
    finish_sweep(2, out_ref)
    for direction in range(4):
        sent(*fine_message(2, direction))


def solution(mesh):
    sec_count, dom_count = mesh.shape["sec"], mesh.shape["dom"]

    def on_device(defect, point_inverse, flux_jacobian, time_term, penalty, element_inverse):
        def run(*refs):
            kernel(sec_count, dom_count, *refs)

        vmem = lambda *shape: pltpu.VMEM(shape + (8, 128), F32)
        dma = lambda *shape: pltpu.SemaphoreType.DMA(shape)
        out = pl.pallas_call(
            run,
            out_shape=jax.ShapeDtypeStruct((5, 4, 4, 2, 8, 128), F32),
            in_specs=[pl.BlockSpec(memory_space=pltpu.HBM)] * 6,
            out_specs=pl.BlockSpec(memory_space=pltpu.VMEM),
            scratch_shapes=[
                vmem(5, 4, 4, 2), vmem(5, 5, 4, 4, 2), pltpu.VMEM((75, 4, 128), F32), pltpu.VMEM((4, 128), F32),
                pltpu.VMEM((3, 4, 128), F32), pltpu.VMEM((25, 4, 128), F32),
                vmem(5, 4, 4, 2), vmem(100), vmem(104), vmem(2, 4, 2), vmem(5, 4, 4, 2),
                vmem(3, 4, 5, 2), vmem(3, 4, 5, 2), vmem(4, 26), vmem(4, 26),
                vmem(2, 4, 15), vmem(2, 4, 15), vmem(2, 4, 6), vmem(2, 4, 6), vmem(4, 13), vmem(4, 13),
                vmem(2, 104), vmem(2, 3), vmem(2, 40), vmem(2, 40), vmem(2, 48), vmem(2, 5, 8), vmem(2, 3, 5, 4),
                vmem(20), vmem(20), vmem(2, 2, 5), vmem(120),
                dma(3, 4), dma(3, 4), dma(8), dma(8), dma(2, 8), dma(2, 8), dma(9),
            ],
            compiler_params=pltpu.CompilerParams(
                collective_id=0, has_side_effects=True, vmem_limit_bytes=48 << 20
            ),
        )(
            *(
                pltpu.with_memory_space_constraint(array, pltpu.HBM)
                for array in (
                    defect.reshape(5, 4, 4, 2, 8, 128),
                    point_inverse.reshape(5, 5, 4, 4, 2, 8, 128),
                    flux_jacobian.reshape(75, 4, 128),
                    time_term,
                    penalty,
                    element_inverse.reshape(25, 4, 128),
                )
            )
        )
        return out.reshape(5, 64, 4, 128)

    placed = (
        P(None, None, "sec", "dom"),
        P(None, None, None, "sec", "dom"),
        P(None, None, None, "sec", "dom"),
        P("sec", "dom"),
        P(None, "sec", "dom"),
        P(None, None, "sec", "dom"),
    )
    return jax.shard_map(
        on_device,
        mesh=mesh,
        in_specs=placed,
        out_specs=P(None, None, "sec", "dom"),
        check_vma=False,
    )
```
